512 devices in a mesh: src: 16 (over y, x_lo, core), gz: 32 (over x_hi, z).
Axes of the slice: x: 4 (x_hi: 2, x_lo: 2; x = x_hi * 2 + x_lo), y: 4, z: 16, core: 2. Of those that a mesh axis runs over, the one named last changes fastest.
Arguments:
- conductivity: float32 [128, 128, 128], P('gz'), may hold values from 0.2 to 5
- perturbation: float32 [128, 128, 128], P('gz'), may hold values from -6 to 6
- fields: float32 [32, 128, 128, 128], P('src', 'gz'), may hold values from -6 to 6
- increment_start: float32 [32, 128, 128, 128], P('src', 'gz'), may hold values from -3 to 3
- adjoint_start: float32 [32, 128, 128, 128], P('src', 'gz'), may hold values from -0.625 to 0.625
- receivers: int32 [32, 512, 2], P('src'), may hold values from 0 to 2097151
- dipole_weight: float32 [32, 512], P('src'), may hold values from 0.5 to 2
Outputs:
- hessian_product: float32 [128, 128, 128], P('gz', 'src')
- increment: float32 [32, 128, 128, 128], P('src', 'gz')
The draws below stay inside these ranges and needn't reach their ends.
All inputs are finite; a program needn't handle non-finite values.
Results may differ from the reference program's by a relative error of at most 0.0003.
Values sent between devices are 32-bit elements; how exact they have to be, the bound alone decides.
A program may use at most 64 MiB of HBM per device.

```python
import math
import jax
import jax.numpy as jnp
from jax import lax

NX = 128
NY = 128
DIPOLES = 512
SWEEPS = 2
NZ = 128
SOURCES = 32


def with_ends(values, own_key, smallest, high):
    spot = [jax.random.randint(jax.random.fold_in(own_key, axis), (), 0, length) for axis, length in enumerate(values.shape)]
    widest = values.shape.index(max(values.shape))
    beside = spot[:widest] + [(spot[widest] + 1) % values.shape[widest]] + spot[widest + 1:]
    return values.at[tuple(spot)].set(smallest).at[tuple(beside)].set(high)


def shard_levels(key, shape, pieces, smallest, largest):
    gain, own = 1.0, jax.random.fold_in(key, 6)
    for dim, blocks in pieces:
        heights = jnp.exp(jax.random.uniform(jax.random.fold_in(own, dim), (blocks,), jnp.float32, smallest / len(pieces), largest / len(pieces)))
        gain = gain * jnp.repeat(heights, shape[dim] // blocks).reshape([-1 if axis == dim else 1 for axis in range(len(shape))])
    return gain


def normal_values(rng, dims, deviation, reach, split=(), held_as=jnp.bfloat16):
    values = jax.random.normal(rng, dims, jnp.float32) * deviation
    if len(split) > 0:
        values = shard_levels(rng, dims, split, -0.22, 0.18) * values
    return jnp.clip(values, min=-reach, max=reach).astype(held_as)


def setup_inputs(seed: int = 0) -> dict:
    keys = jax.random.split(jax.random.key(seed), 8)
    conductivity = jnp.clip(jnp.exp(math.log(5.0) - 3.218876 * jax.random.uniform(keys[0], (NZ, NX, NY), jnp.float32) ** shard_levels(keys[0], (NZ, NX, NY), ((0, 32),), -0.2, 0.2)), 0.2, 5.0)
    perturbation = normal_values(keys[1], (NZ, NX, NY), 1.0, 6.0, ((0, 32),), jnp.float32)
    fields = normal_values(keys[2], (SOURCES, NZ, NX, NY), 1.0, 6.0, ((0, 16), (1, 32)), jnp.float32)
    increment_start = normal_values(keys[3], (SOURCES, NZ, NX, NY), 0.5, 3.0, ((0, 16), (1, 32)), jnp.float32)
    adjoint_start = normal_values(keys[4], (SOURCES, NZ, NX, NY), 0.1, 0.625, ((0, 16), (1, 32)), jnp.float32)
    receivers = with_ends(jax.random.randint(keys[5], (SOURCES, DIPOLES, 2), 0, NX * NY * NZ), jax.random.fold_in(keys[5], 1), 0, (NX * NY * NZ) - 1).astype(jnp.int32)
    dipole_weight = jnp.clip(jnp.exp(math.log(2.0) - 1.3862944 * jax.random.uniform(keys[6], (SOURCES, DIPOLES), jnp.float32) ** shard_levels(keys[6], (SOURCES, DIPOLES), ((0, 16),), -0.2, 0.2)), 0.5, 2.0)
    return {"conductivity": conductivity, "perturbation": perturbation, "fields": fields, "increment_start": increment_start, "adjoint_start": adjoint_start, "receivers": receivers, "dipole_weight": dipole_weight}


LEAKAGE = 0.5
RELAXATION = 0.8
REGULARIZE = 0.05


def stencil_sides(array):
    widths = [(0, 0)] * (array.ndim - 2) + [(1, 1), (1, 1)]
    padded = jnp.pad(array, widths)
    center = padded[..., 1:-1, 1:-1, 1:-1]
    neighbours = [padded[..., 2:, 1:-1, 1:-1], padded[..., :-2, 1:-1, 1:-1],
                  padded[..., 1:-1, 2:, 1:-1], padded[..., 1:-1, :-2, 1:-1],
                  padded[..., 1:-1, 1:-1, 2:], padded[..., 1:-1, 1:-1, :-2]]
    return center, neighbours


def operate(sigma_pad, field_pad):
    sig_center, sig_near = stencil_sides(sigma_pad)
    fld_center, fld_near = stencil_sides(field_pad)
    result = LEAKAGE * sig_center * fld_center
    for sig_other, fld_other in zip(sig_near, fld_near):
        result = result + 0.5 * (sig_center + sig_other) * (fld_center - fld_other)
    return result


def diagonal(sigma_pad):
    sig_center, sig_near = stencil_sides(sigma_pad)
    result = LEAKAGE * sig_center
    for sig_other in sig_near:
        result = result + 0.5 * (sig_center + sig_other)
    return result


def correlate(adjoint_pad, field_pad):
    adj_center, adj_near = stencil_sides(adjoint_pad)
    fld_center, fld_near = stencil_sides(field_pad)
    result = LEAKAGE * adj_center * fld_center
    for adj_other, fld_other in zip(adj_near, fld_near):
        result = result + 0.5 * (adj_center - adj_other) * (fld_center - fld_other)
    return result


def laplacian(pert_pad):
    center, neighbours = stencil_sides(pert_pad)
    result = center - neighbours[0]
    for other in neighbours[1:]:
        result = result + (center - other)
    return result


def pad_depth(array):
    widths = [(0, 0)] * (array.ndim - 3) + [(1, 1), (0, 0), (0, 0)]
    return jnp.pad(array, widths)


def reference(conductivity, perturbation, fields, increment_start, adjoint_start, receivers, dipole_weight):
    sig_pad = pad_depth(conductivity)
    pert_pad = pad_depth(perturbation)
    diag_all = diagonal(sig_pad)

    def per_source(running, element):
        field, first_guess, adjoint_guess, electrodes, weight = element
        field_pad = pad_depth(field)
        source_term = -operate(pert_pad, field_pad)
        increment = first_guess
        for sweep_index in range(SWEEPS):
            increment = increment + RELAXATION * (source_term - operate(sig_pad, pad_depth(increment))) / diag_all
        cells = increment.reshape(-1)
        first = electrodes[:, 0].astype(jnp.int32)
        second = electrodes[:, 1].astype(jnp.int32)
        reading = weight * (cells[first] - cells[second])
        adjoint_source = jnp.zeros_like(cells).at[first].add(reading).at[second].add(-reading)
        adjoint_source = adjoint_source.reshape(increment.shape)
        adjoint = adjoint_guess
        for sweep_index in range(SWEEPS):
            adjoint = adjoint + RELAXATION * (adjoint_source - operate(sig_pad, pad_depth(adjoint))) / diag_all
        return running + correlate(pad_depth(adjoint), field_pad), increment

    start = jnp.zeros(conductivity.shape, jnp.float32)
    summed, increments = lax.scan(per_source, start, (fields, increment_start, adjoint_start, receivers, dipole_weight))
    return -summed + REGULARIZE * laplacian(pert_pad), increments
```

```python
import functools

import jax
import jax.numpy as jnp
from jax import lax
from jax.experimental import pallas as pl
from jax.experimental.pallas import tpu as pltpu
from jax.sharding import PartitionSpec as P

LEAKAGE = 0.5
RELAXATION = 0.8
REGULARIZE = 0.05
KEEP = 1.0 - RELAXATION
MESH = pl.DeviceIdType.MESH
DMA = pltpu.SemaphoreType.DMA
QUARTER = 4


def ahead(plane, axis):
    return pltpu.roll(plane, plane.shape[axis] - 1, axis)


def behind(plane, axis):
    return pltpu.roll(plane, 1, axis)


def kernel(
    sigma_hbm, pert_hbm, field_hbm, start_hbm, adjoint_hbm, cells_ref, weight_ref,
    hess_ref, inc_hbm,
    sg, pe, fe, ie, i1, o2, ae, a1, a2, b1,
    coef, ew, nb, st, vh, ns, lap,
    hot, spot, read, got_a, part, got_b, co, rb,
    in_sem, out_sem, z_send, z_recv, a_send, a_recv, b_send, b_recv, s_send, s_recv,
):
    src, gz = lax.axis_index("src"), lax.axis_index("gz")
    n_src, n_gz = lax.axis_size("src"), lax.axis_size("gz")
    sources, depth, nx, ny = field_hbm.shape
    dipoles = weight_ref.shape[1]
    has_lo, has_hi = gz > 0, gz < n_gz - 1
    row = lax.broadcasted_iota(jnp.int32, (nx, ny), 0)
    col = lax.broadcasted_iota(jnp.int32, (nx, ny), 1)
    inside = {(0, 1): row < nx - 1, (0, -1): row > 0, (1, 1): col < ny - 1, (1, -1): col > 0}
    sides = tuple(inside)

    def shifted(plane, side):
        return ahead(plane, side[0]) if side[1] > 0 else behind(plane, side[0])

    def neighbour(plane, side):
        return jnp.where(inside[side], shifted(plane, side), 0.0)

    lo, hi = (src, gz - 1), (src, gz + 1)
    half = n_gz // 2
    x_part, z_part = gz // half, lax.rem(gz, half)
    z_group, z_in = z_part // QUARTER, lax.rem(z_part, QUARTER)
    groups = half // QUARTER
    near = []
    for dx in range(2):
        for dz in range(QUARTER):
            if dx or dz:
                near.append((src, lax.rem(x_part + dx, 2) * half + z_group * QUARTER + lax.rem(z_in + dz, QUARTER)))
    far = [(src, x_part * half + lax.rem(z_group + d, groups) * QUARTER + z_in) for d in range(1, groups)]
    mates = [(lax.rem(src + d, n_src), gz) for d in range(1, n_src)]

    barrier = pltpu.get_barrier_semaphore()

    def signal(device):
        pl.semaphore_signal(barrier, inc=1, device_id=device, device_id_type=MESH)

    pl.when(has_lo)(lambda: signal(lo))
    pl.when(has_hi)(lambda: signal(hi))
    for device in near + far + mates:
        signal(device)

    loads = [
        pltpu.make_async_copy(sigma_hbm, sg.at[pl.ds(3, depth)], in_sem.at[0]),
        pltpu.make_async_copy(pert_hbm, pe.at[pl.ds(1, depth)], in_sem.at[1]),
        pltpu.make_async_copy(start_hbm, ie.at[:, pl.ds(1, depth)], in_sem.at[2]),
        pltpu.make_async_copy(field_hbm, fe.at[:, pl.ds(1, depth)], in_sem.at[3]),
        pltpu.make_async_copy(adjoint_hbm, ae.at[:, pl.ds(3, depth)], in_sem.at[4]),
    ]
    for load in loads:
        load.start()

    empty = jnp.zeros((nx, ny), jnp.float32)

    def clear(high):
        for i in range(3):
            sg[depth + 3 + i if high else i] = empty
            for s in range(sources):
                ae[s, depth + 3 + i if high else i] = empty
        e = depth + 1 if high else 0
        pe[e] = empty
        for s in range(sources):
            fe[s, e] = empty
            ie[s, e] = empty
            vh[1 if high else 0, s] = empty

    pl.when(jnp.logical_not(has_lo))(lambda: clear(False))
    pl.when(jnp.logical_not(has_hi))(lambda: clear(True))

    def edge(index, up_src, up_dst, down_src, down_dst):
        up = pltpu.make_async_remote_copy(
            src_ref=up_src, dst_ref=up_dst, send_sem=z_send.at[0, index], recv_sem=z_recv.at[0, index],
            device_id=hi, device_id_type=MESH)
        down = pltpu.make_async_remote_copy(
            src_ref=down_src, dst_ref=down_dst, send_sem=z_send.at[1, index], recv_sem=z_recv.at[1, index],
            device_id=lo, device_id_type=MESH)
        return up, down

    def begin(pair):
        pl.when(has_hi)(pair[0].start)
        pl.when(has_lo)(pair[1].start)

    def sent(pair):
        pl.when(has_hi)(pair[0].wait_send)
        pl.when(has_lo)(pair[1].wait_send)

    def arrived(pair):
        pl.when(has_lo)(pair[0].wait_recv)
        pl.when(has_hi)(pair[1].wait_recv)

    edge_sigma = edge(0, sg.at[pl.ds(depth, 3)], sg.at[pl.ds(0, 3)], sg.at[pl.ds(3, 3)], sg.at[pl.ds(depth + 3, 3)])
    edge_pert = edge(1, pe.at[depth], pe.at[0], pe.at[1], pe.at[depth + 1])
    edge_start = edge(2, ie.at[:, depth], ie.at[:, 0], ie.at[:, 1], ie.at[:, depth + 1])
    edge_field = edge(3, fe.at[:, depth], fe.at[:, 0], fe.at[:, 1], fe.at[:, depth + 1])
    edge_value = edge(4, nb.at[:, depth - 1], vh.at[0], nb.at[:, 0], vh.at[1])
    edge_adj = edge(5, ae.at[:, pl.ds(depth, 3)], ae.at[:, pl.ds(0, 3)], ae.at[:, pl.ds(3, 3)], ae.at[:, pl.ds(depth + 3, 3)])

    for load in loads:
        load.wait()
    pl.semaphore_wait(barrier, len(near) + len(far) + len(mates) + has_lo.astype(jnp.int32) + has_hi.astype(jnp.int32))

    begin(edge_sigma)
    begin(edge_pert)
    begin(edge_start)
    begin(edge_field)

    def local(k, carry):
        below, above = jnp.maximum(k - 1, 0), jnp.minimum(k + 1, depth - 1)
        has_below, has_above = (k > 0).astype(jnp.float32), (k < depth - 1).astype(jnp.float32)
        sig, pert = sg[k + 3], pe[k + 1]
        sig_z = [has_below * 0.5 * (sig + sg[below + 3]), has_above * 0.5 * (sig + sg[above + 3])]
        pert_z = [has_below * 0.5 * (pert + pe[below + 1]), has_above * 0.5 * (pert + pe[above + 1])]
        near_pert = [neighbour(pert, side) for side in sides]
        sig_w = [jnp.where(inside[side], 0.5 * (sig + shifted(sig, side)), 0.0) for side in sides]
        pert_w = [jnp.where(inside[side], 0.5 * (pert + other), 0.0) for side, other in zip(sides, near_pert)]
        pert_sum = (near_pert[0] + near_pert[1]) + (near_pert[2] + near_pert[3])
        diag = LEAKAGE * pert + 2.0 * pert + 0.5 * pert_sum + pert_z[0] + pert_z[1]
        for s in range(sources):
            field, start = fe[s, k + 1], ie[s, k + 1]
            term = pert_z[0] * fe[s, below + 1] + pert_z[1] * fe[s, above + 1] - diag * field
            near_field = empty
            for side, weight in zip(sides, pert_w):
                other = neighbour(field, side)
                term = term + weight * other
                near_field = near_field + other
            st[s, k] = term
            ns[s, k] = near_field
            total = term + sig_z[0] * ie[s, below + 1] + sig_z[1] * ie[s, above + 1]
            for side, weight in zip(sides, sig_w):
                total = total + weight * shifted(start, side)
            nb[s, k] = total
        lap[:, k] = (4.0 * pert - pert_sum).reshape(n_src, nx // n_src, ny)
        return carry

    lax.fori_loop(0, depth, local, 0)
    begin(edge_value)

    def electrodes(s):
        both = cells_ref[s]
        flat = jnp.concatenate([both[0:1], both[1:2]], axis=1)
        plane_row = flat // ny
        return plane_row - (gz * depth - 2) * nx, flat - plane_row * ny

    def mark(s):
        rows, columns = electrodes(s)
        spot_s = jnp.broadcast_to(columns, (ny, 2 * dipoles)) == lax.broadcasted_iota(jnp.int32, (ny, 2 * dipoles), 0)
        spot_s = jnp.where(spot_s, 1.0, 0.0).astype(jnp.bfloat16)
        for piece in range(3):
            spot[s, pl.ds(piece * ny, ny)] = spot_s

        def chunk(c, carry):
            index = lax.broadcasted_iota(jnp.int32, (nx, 2 * dipoles), 0) + c * nx
            match = jnp.broadcast_to(rows, (nx, 2 * dipoles)) == index
            hot[s, pl.ds(pl.multiple_of(c * nx, nx), nx)] = jnp.where(match, 1.0, 0.0).astype(jnp.bfloat16)
            return carry

        lax.fori_loop(0, depth + 4, chunk, 0)

    for s in range(sources):
        mark(s)

    arrived(edge_sigma)

    def coefficients(e, carry):
        sig, below, above = sg[e + 1], sg[e], sg[e + 2]
        others = [neighbour(sig, side) for side in sides]
        diag = (LEAKAGE + 3.0) * sig + 0.5 * (((others[0] + others[1]) + (others[2] + others[3])) + (below + above))
        plane = gz * depth + e - 2
        exists = jnp.logical_and(plane >= 0, plane < n_gz * depth)
        scale = jnp.where(exists, RELAXATION / diag, 0.0)
        ew[e] = scale
        scale = 0.5 * scale
        for i, side in enumerate(sides):
            coef[i, e] = jnp.where(inside[side], scale * (sig + others[i]), 0.0)
        coef[4, e] = scale * (sig + below)
        coef[5, e] = scale * (sig + above)
        return carry

    lax.fori_loop(0, depth + 4, coefficients, 0)

    def around(e, values, s, offset):
        v = e - offset
        center = values[s, v]
        total = coef[4, e] * values[s, v - 1] + coef[5, e] * values[s, v + 1]
        for i, side in enumerate(sides):
            total = total + coef[i, e] * shifted(center, side)
        return center, total

    sent(edge_sigma)
    sent(edge_pert)
    sent(edge_start)
    sent(edge_field)
    sent(edge_value)
    begin(edge_adj)
    arrived(edge_pert)
    arrived(edge_start)
    arrived(edge_field)
    arrived(edge_value)

    for k in range(1, depth - 1):
        for s in range(sources):
            i1[s, k + 1] = KEEP * ie[s, k + 1] + ew[k + 2] * nb[s, k]
    for own, other, v in ((0, -1, 0), (depth - 1, depth, 1)):
        sig_w = 0.5 * (sg[own + 3] + sg[other + 3])
        pert_w = 0.5 * (pe[own + 1] + pe[other + 1])
        lap[:, own] = lap[:, own] + (pe[own + 1] - pe[other + 1]).reshape(n_src, nx // n_src, ny)
        for s in range(sources):
            face = pert_w * (fe[s, other + 1] - fe[s, own + 1])
            st[s, own] = st[s, own] + face
            i1[s, own + 1] = KEEP * ie[s, own + 1] + ew[own + 2] * (nb[s, own] + face + sig_w * ie[s, other + 1])
            i1[s, other + 1] = KEEP * ie[s, other + 1] + ew[other + 2] * (vh[v, s] - face + sig_w * ie[s, own + 1])
    for k in range(depth - 1):
        face = (pe[k + 1] - pe[k + 2]).reshape(n_src, nx // n_src, ny)
        lap[:, k] = lap[:, k] + face
        lap[:, k + 1] = lap[:, k + 1] - face

    def second(k, carry):
        for s in range(sources):
            center, total = around(k + 2, i1, s, 1)
            o2[s, k] = KEEP * center + ew[k + 2] * st[s, k] + total
        return carry

    lax.fori_loop(0, depth, second, 0)
    store = pltpu.make_async_copy(o2, inc_hbm, out_sem)
    store.start()

    def pick(s):
        rows, _ = electrodes(s)
        value = o2[s].reshape(depth * nx, ny)
        high = value.astype(jnp.bfloat16)
        rest = value - high.astype(jnp.float32)
        middle = rest.astype(jnp.bfloat16)
        low = (rest - middle.astype(jnp.float32)).astype(jnp.bfloat16)
        columns = jnp.dot(
            jnp.concatenate([high, middle, low], axis=1), spot[s], preferred_element_type=jnp.float32)
        index = lax.broadcasted_iota(jnp.int32, columns.shape, 0) + 2 * nx
        picked = jnp.sum(jnp.where(jnp.broadcast_to(rows, columns.shape) == index, columns, 0.0), axis=0, keepdims=True)
        reading = picked[:, :dipoles] - picked[:, dipoles:]
        for i in range(dipoles // 128):
            read[pl.ds(s * (dipoles // 128) + i, 1)] = reading[:, i * 128:(i + 1) * 128]

    for s in range(sources):
        pick(s)

    def spread(devices, source, target, send, recv):
        copies = []
        for i, device in enumerate(devices):
            copies.append(pltpu.make_async_remote_copy(
                src_ref=source(i), dst_ref=target.at[i], send_sem=send.at[i], recv_sem=recv.at[i],
                device_id=device, device_id_type=MESH))
            copies[-1].start()
        return copies

    near_copies = spread(near, lambda i: read, got_a, a_send, a_recv)

    def across(k, carry):
        for s in range(sources):
            ns[s, k] = ns[s, k] + (fe[s, k] + fe[s, k + 2])
        return carry

    lax.fori_loop(0, depth, across, 0)

    total = read[...]
    for i, copy in enumerate(near_copies):
        copy.wait_recv()
        total = total + got_a[i]
    part[...] = total
    far_copies = spread(far, lambda i: part, got_b, b_send, b_recv)

    arrived(edge_adj)

    def adjoint_first(e, carry):
        for s in range(sources):
            center, total = around(e, ae, s, -1)
            a1[s, e] = KEEP * center + total
        return carry

    lax.fori_loop(0, depth + 4, adjoint_first, 0)

    def adjoint_second(e, carry):
        for s in range(sources):
            center, total = around(e, a1, s, 0)
            a2[s, e - 1] = KEEP * center + total
        return carry

    lax.fori_loop(1, depth + 3, adjoint_second, 0)

    total = part[...]
    for i, copy in enumerate(far_copies):
        copy.wait_recv()
        total = total + got_b[i]
    for copy in near_copies + far_copies:
        copy.wait_send()
    read[...] = total

    def scatter(s):
        per = dipoles // 128
        value = jnp.concatenate([read[pl.ds(s * per + i, 1)] for i in range(per)], axis=1) * weight_ref[pl.ds(s, 1)]
        value = jnp.concatenate([value, -value], axis=1)
        high = value.astype(jnp.bfloat16)
        low = (value - high.astype(jnp.float32)).astype(jnp.bfloat16)
        pieces = jnp.concatenate([spot[s, pl.ds(0, ny)] * high, spot[s, pl.ds(0, ny)] * low], axis=0)
        placed = lax.dot_general(hot[s], pieces, (((1,), (1,)), ((), ())), preferred_element_type=jnp.float32)
        placed = (placed[:, :ny] + placed[:, ny:]).reshape(depth + 4, nx, ny)
        b1[s] = ew[...] * placed

    for s in range(sources):
        scatter(s)

    def adjoint_readings(e, carry):
        for s in range(sources):
            center, total = around(e, b1, s, 0)
            a2[s, e - 1] = a2[s, e - 1] + (1.0 + KEEP) * center + total
        return carry

    lax.fori_loop(1, depth + 3, adjoint_readings, 0)

    def correlate(k, carry):
        product = empty
        mixed = empty
        for s in range(sources):
            adj, field = a2[s, k + 1], fe[s, k + 1]
            near_adj = a2[s, k] + a2[s, k + 2]
            for side in sides:
                near_adj = near_adj + neighbour(adj, side)
            product = product + adj * field
            mixed = mixed + (adj * ns[s, k] + field * near_adj)
            mixed = mixed - (a2[s, k] * fe[s, k] + a2[s, k + 2] * fe[s, k + 2])
        around_product = empty
        for side in sides:
            around_product = around_product + neighbour(product, side)
        result = (LEAKAGE + 3.0) * product + 0.5 * (around_product - mixed)
        co[:, k] = result.reshape(n_src, nx // n_src, ny)
        return carry

    lax.fori_loop(0, depth, correlate, 0)

    mate_copies = spread(mates, lambda i: co.at[mates[i][0]], rb, s_send, s_recv)
    total = co[src]
    for i, copy in enumerate(mate_copies):
        copy.wait_recv()
        total = total + rb[i]
    hess_ref[...] = REGULARIZE * lap[src] - total

    sent(edge_adj)
    for copy in mate_copies:
        copy.wait_send()
    store.wait()


def on_device(conductivity, perturbation, fields, increment_start, adjoint_start, receivers, dipole_weight):
    sources, depth, nx, ny = fields.shape
    dipoles = dipole_weight.shape[1]
    n_src, n_gz = lax.axis_size("src"), lax.axis_size("gz")
    share = nx // n_src
    rows = sources * dipoles // 128

    def planes(*lead):
        return pltpu.VMEM((*lead, nx, ny), jnp.float32)

    near, far, mates = 2 * QUARTER - 1, n_gz // 2 // QUARTER - 1, n_src - 1
    scratch = [
        planes(depth + 6), planes(depth + 2), planes(sources, depth + 2), planes(sources, depth + 2),
        planes(sources, depth + 2), planes(sources, depth), planes(sources, depth + 6), planes(sources, depth + 4),
        planes(sources, depth + 2), planes(sources, depth + 4),
        planes(6, depth + 4), planes(depth + 4), planes(sources, depth), planes(sources, depth),
        planes(2, sources), planes(sources, depth), pltpu.VMEM((n_src, depth, share, ny), jnp.float32),
        pltpu.VMEM((sources, (depth + 4) * nx, 2 * dipoles), jnp.bfloat16),
        pltpu.VMEM((sources, 3 * ny, 2 * dipoles), jnp.bfloat16),
        pltpu.VMEM((rows, 128), jnp.float32), pltpu.VMEM((near, rows, 128), jnp.float32),
        pltpu.VMEM((rows, 128), jnp.float32), pltpu.VMEM((far, rows, 128), jnp.float32),
        pltpu.VMEM((n_src, depth, share, ny), jnp.float32), pltpu.VMEM((mates, depth, share, ny), jnp.float32),
        DMA((5,)), DMA, DMA((2, 6)), DMA((2, 6)), DMA((near,)), DMA((near,)), DMA((far,)), DMA((far,)),
        DMA((mates,)), DMA((mates,)),
    ]
    anywhere = pl.BlockSpec(memory_space=pl.ANY)
    vmem = pl.BlockSpec(memory_space=pltpu.VMEM)
    return pl.pallas_call(
        kernel,
        out_shape=(
            jax.ShapeDtypeStruct((depth, share, ny), jnp.float32),
            jax.ShapeDtypeStruct(increment_start.shape, jnp.float32),
        ),
        in_specs=[anywhere] * 5 + [vmem] * 2,
        out_specs=(vmem, anywhere),
        scratch_shapes=scratch,
        compiler_params=pltpu.CompilerParams(
            collective_id=0, has_side_effects=True, vmem_limit_bytes=48 * 2**20),
    )(conductivity, perturbation, fields, increment_start, adjoint_start, jnp.swapaxes(receivers, 1, 2), dipole_weight)


def solution(mesh):
    return jax.shard_map(
        on_device,
        mesh=mesh,
        in_specs=(
            P("gz", None, None),
            P("gz", None, None),
            P("src", "gz", None, None),
            P("src", "gz", None, None),
            P("src", "gz", None, None),
            P("src", None, None),
            P("src", None),
        ),
        out_specs=(P("gz", "src", None), P("src", "gz", None, None)),
        check_vma=False,
    )
```

```python
import functools

import jax
import jax.numpy as jnp
from jax import lax
from jax.experimental import pallas as pl
from jax.experimental.pallas import tpu as pltpu
from jax.sharding import PartitionSpec as P

LEAKAGE = 0.5
RELAXATION = 0.8
REGULARIZE = 0.05
KEEP = 1.0 - RELAXATION
MESH = pl.DeviceIdType.MESH
DMA = pltpu.SemaphoreType.DMA


def ahead(plane, axis):
    return pltpu.roll(plane, plane.shape[axis] - 1, axis)


def behind(plane, axis):
    return pltpu.roll(plane, 1, axis)


def kernel(
    sigma_hbm, pert_hbm, field_hbm, start_hbm, adjoint_hbm, cells_hbm, weight_hbm,
    hess_ref, inc_hbm,
    cells_ref, weight_ref, sg, pe, fe, ie, i1, i2, o2, ae, a1, a2, b1,
    coef, ew, nb, st, vh, ns, lap,
    hot, spot, read, got, co, rb,
    in_sem, out_sem, known, z_send, z_recv, r_send, r_recv, s_send, s_recv,
):
    src, gz = lax.axis_index("src"), lax.axis_index("gz")
    n_src, n_gz = lax.axis_size("src"), lax.axis_size("gz")
    sources, depth, nx, ny = field_hbm.shape
    dipoles = weight_ref.shape[1]
    has_lo, has_hi = gz > 0, gz < n_gz - 1
    row = lax.broadcasted_iota(jnp.int32, (nx, ny), 0)
    col = lax.broadcasted_iota(jnp.int32, (nx, ny), 1)
    inside = {(0, 1): row < nx - 1, (0, -1): row > 0, (1, 1): col < ny - 1, (1, -1): col > 0}
    sides = tuple(inside)

    def shifted(plane, side):
        return ahead(plane, side[0]) if side[1] > 0 else behind(plane, side[0])

    def neighbour(plane, side):
        return jnp.where(inside[side], shifted(plane, side), 0.0)

    lo, hi = (src, gz - 1), (src, gz + 1)
    half = n_gz // 2
    x_part, z_part = gz // half, lax.rem(gz, half)

    def at(dx, dz):
        return (src, lax.rem(x_part + dx, 2) * half + lax.rem(z_part + dz + half, half))

    steps = sorted(range(half), key=lambda dz: -min(dz, half - dz))
    others = [at(dx, dz) for dz in steps for dx in (1, 0) if dx or dz]
    mates = [(lax.rem(src + d, n_src), gz) for d in range(1, n_src)]

    barrier = pltpu.get_barrier_semaphore()

    def signal(device, semaphore=barrier):
        pl.semaphore_signal(semaphore, inc=1, device_id=device, device_id_type=MESH)

    greeted = [at(0, 1), at(0, -1), at(1, 0), *mates]
    joint = jnp.logical_or(gz == half - 1, gz == half)
    for device in greeted:
        signal(device)
    pl.when(joint)(lambda: signal((src, n_gz - 1 - gz)))

    rounds = [[at(0, 1), at(0, -1)], [at(0, 2), at(0, -2)], [at(0, 4), at(0, -4)], [at(1, 0)]]

    def tell(i):
        for device in rounds[i]:
            signal(device, known.at[i])

    def meet(i):
        pl.semaphore_wait(known.at[i], len(rounds[i]))

    loads = [
        pltpu.make_async_copy(sigma_hbm, sg.at[pl.ds(3, depth)], in_sem.at[0]),
        pltpu.make_async_copy(pert_hbm, pe.at[pl.ds(1, depth)], in_sem.at[1]),
        pltpu.make_async_copy(start_hbm, ie.at[:, pl.ds(1, depth)], in_sem.at[2]),
        pltpu.make_async_copy(field_hbm, fe.at[:, pl.ds(1, depth)], in_sem.at[3]),
        pltpu.make_async_copy(adjoint_hbm, ae.at[:, pl.ds(3, depth)], in_sem.at[4]),
        pltpu.make_async_copy(cells_hbm, cells_ref, in_sem.at[5]),
        pltpu.make_async_copy(weight_hbm, weight_ref, in_sem.at[6]),
    ]
    for load in loads:
        load.start()

    empty = jnp.zeros((nx, ny), jnp.float32)

    def clear(high):
        for i in range(3):
            sg[depth + 3 + i if high else i] = empty
            for s in range(sources):
                ae[s, depth + 3 + i if high else i] = empty
        e = depth + 1 if high else 0
        pe[e] = empty
        for s in range(sources):
            fe[s, e] = empty
            ie[s, e] = empty
            vh[1 if high else 0, s] = empty

    pl.when(jnp.logical_not(has_lo))(lambda: clear(False))
    pl.when(jnp.logical_not(has_hi))(lambda: clear(True))

    def edge(index, up_src, up_dst, down_src, down_dst):
        up = pltpu.make_async_remote_copy(
            src_ref=up_src, dst_ref=up_dst, send_sem=z_send.at[0, index], recv_sem=z_recv.at[0, index],
            device_id=hi, device_id_type=MESH)
        down = pltpu.make_async_remote_copy(
            src_ref=down_src, dst_ref=down_dst, send_sem=z_send.at[1, index], recv_sem=z_recv.at[1, index],
            device_id=lo, device_id_type=MESH)
        return up, down

    def begin(pair):
        pl.when(has_hi)(pair[0].start)
        pl.when(has_lo)(pair[1].start)

    def sent(pair):
        pl.when(has_hi)(pair[0].wait_send)
        pl.when(has_lo)(pair[1].wait_send)

    def arrived(pair):
        pl.when(has_lo)(pair[0].wait_recv)
        pl.when(has_hi)(pair[1].wait_recv)

    edge_sigma = edge(0, sg.at[pl.ds(depth, 3)], sg.at[pl.ds(0, 3)], sg.at[pl.ds(3, 3)], sg.at[pl.ds(depth + 3, 3)])
    edge_pert = edge(1, pe.at[depth], pe.at[0], pe.at[1], pe.at[depth + 1])
    edge_start = edge(2, ie.at[:, depth], ie.at[:, 0], ie.at[:, 1], ie.at[:, depth + 1])
    edge_field = edge(3, fe.at[:, depth], fe.at[:, 0], fe.at[:, 1], fe.at[:, depth + 1])
    edge_value = edge(4, nb.at[:, depth - 1], vh.at[0], nb.at[:, 0], vh.at[1])
    edge_adj = edge(5, ae.at[:, pl.ds(depth, 3)], ae.at[:, pl.ds(0, 3)], ae.at[:, pl.ds(3, 3)], ae.at[:, pl.ds(depth + 3, 3)])

    for load in loads:
        load.wait()
    pl.semaphore_wait(barrier, len(greeted) + joint.astype(jnp.int32))

    begin(edge_sigma)
    begin(edge_pert)
    tell(0)

    def local(k, carry):
        below, above = jnp.maximum(k - 1, 0), jnp.minimum(k + 1, depth - 1)
        has_below, has_above = (k > 0).astype(jnp.float32), (k < depth - 1).astype(jnp.float32)
        sig, pert = sg[k + 3], pe[k + 1]
        sig_z = [has_below * 0.5 * (sig + sg[below + 3]), has_above * 0.5 * (sig + sg[above + 3])]
        pert_z = [has_below * 0.5 * (pert + pe[below + 1]), has_above * 0.5 * (pert + pe[above + 1])]
        near_pert = [neighbour(pert, side) for side in sides]
        sig_w = [jnp.where(inside[side], 0.5 * (sig + shifted(sig, side)), 0.0) for side in sides]
        pert_w = [jnp.where(inside[side], 0.5 * (pert + other), 0.0) for side, other in zip(sides, near_pert)]
        pert_sum = (near_pert[0] + near_pert[1]) + (near_pert[2] + near_pert[3])
        diag = LEAKAGE * pert + 2.0 * pert + 0.5 * pert_sum + pert_z[0] + pert_z[1]
        for s in range(sources):
            field, start = fe[s, k + 1], ie[s, k + 1]
            term = pert_z[0] * fe[s, below + 1] + pert_z[1] * fe[s, above + 1] - diag * field
            near_field = empty
            for side, weight in zip(sides, pert_w):
                other = neighbour(field, side)
                term = term + weight * other
                near_field = near_field + other
            st[s, k + 1] = term
            ns[s, k] = near_field
            total = term + sig_z[0] * ie[s, below + 1] + sig_z[1] * ie[s, above + 1]
            for side, weight in zip(sides, sig_w):
                total = total + weight * shifted(start, side)
            nb[s, k] = total
        lap[:, k] = (4.0 * pert - pert_sum).reshape(n_src, nx // n_src, ny)
        return carry

    lax.fori_loop(0, depth, local, 0)
    meet(0)
    tell(1)

    def electrodes(s):
        both = cells_ref[s]
        flat = jnp.concatenate([both[0:1], both[1:2]], axis=1)
        plane_row = flat // ny
        return plane_row - (gz * depth - 2) * nx, flat - plane_row * ny

    def mark(s):
        rows, columns = electrodes(s)
        spot_s = jnp.broadcast_to(columns, (ny, 2 * dipoles)) == lax.broadcasted_iota(jnp.int32, (ny, 2 * dipoles), 0)
        spot_s = jnp.where(spot_s, 1.0, 0.0).astype(jnp.bfloat16)
        for piece in range(3):
            spot[s, pl.ds(piece * ny, ny)] = spot_s

        def chunk(c, carry):
            index = lax.broadcasted_iota(jnp.int32, (nx, 2 * dipoles), 0) + c * nx
            match = jnp.broadcast_to(rows, (nx, 2 * dipoles)) == index
            hot[s, pl.ds(pl.multiple_of(c * nx, nx), nx)] = jnp.where(match, 1.0, 0.0).astype(jnp.bfloat16)
            return carry

        lax.fori_loop(0, depth + 4, chunk, 0)

    for s in range(sources):
        mark(s)
    meet(1)
    tell(2)
    sent(edge_sigma)
    sent(edge_pert)
    begin(edge_field)
    begin(edge_adj)

    arrived(edge_sigma)

    def coefficients(e, carry):
        sig, below, above = sg[e + 1], sg[e], sg[e + 2]
        others = [neighbour(sig, side) for side in sides]
        diag = (LEAKAGE + 3.0) * sig + 0.5 * (((others[0] + others[1]) + (others[2] + others[3])) + (below + above))
        plane = gz * depth + e - 2
        exists = jnp.logical_and(plane >= 0, plane < n_gz * depth)
        scale = jnp.where(exists, RELAXATION / diag, 0.0)
        ew[e] = scale
        scale = 0.5 * scale
        for i, side in enumerate(sides):
            coef[i, e] = jnp.where(inside[side], scale * (sig + others[i]), 0.0)
        coef[4, e] = scale * (sig + below)
        coef[5, e] = scale * (sig + above)
        return carry

    lax.fori_loop(0, depth + 4, coefficients, 0)

    def around(e, values, s, offset):
        v = e - offset
        center = values[s, v]
        total = coef[4, e] * values[s, v - 1] + coef[5, e] * values[s, v + 1]
        for i, side in enumerate(sides):
            total = total + coef[i, e] * shifted(center, side)
        return center, total

    meet(2)
    tell(3)
    arrived(edge_pert)

    faces = ((0, -1, 0), (depth - 1, depth, 1))

    def face_weights(own, other):
        return 0.5 * (sg[own + 3] + sg[other + 3]), 0.5 * (pe[own + 1] + pe[other + 1])

    for k in range(1, depth - 1):
        for s in range(sources):
            i1[s, k + 2] = KEEP * ie[s, k + 1] + ew[k + 2] * nb[s, k]
    for own, other, v in faces:
        sig_w, pert_w = face_weights(own, other)
        for s in range(sources):
            moved = pert_w * fe[s, own + 1]
            st[s, own + 1] = st[s, own + 1] - moved
            st[s, other + 1] = moved
            i1[s, own + 2] = KEEP * ie[s, own + 1] + ew[own + 2] * (nb[s, own] - moved)
            i1[s, other + 2] = ew[other + 2] * (sig_w * ie[s, own + 1] + moved)
    for s in range(sources):
        i1[s, 0] = empty
        i1[s, depth + 3] = empty

    def second(e, carry):
        for s in range(sources):
            center, total = around(e, i1, s, 0)
            i2[s, e] = KEEP * center + ew[e] * st[s, e - 1] + total
        return carry

    lax.fori_loop(1, depth + 3, second, 0)
    for s in range(sources):
        i2[s, 0] = coef[5, 0] * i1[s, 1]
        i2[s, depth + 3] = coef[4, depth + 3] * i1[s, depth + 2]

    def pick(s):
        rows, _ = electrodes(s)
        value = i2[s].reshape((depth + 4) * nx, ny)
        high = value.astype(jnp.bfloat16)
        rest = value - high.astype(jnp.float32)
        middle = rest.astype(jnp.bfloat16)
        low = (rest - middle.astype(jnp.float32)).astype(jnp.bfloat16)
        columns = jnp.dot(
            jnp.concatenate([high, middle, low], axis=1), spot[s], preferred_element_type=jnp.float32)
        index = lax.broadcasted_iota(jnp.int32, columns.shape, 0)
        picked = jnp.sum(jnp.where(jnp.broadcast_to(rows, columns.shape) == index, columns, 0.0), axis=0, keepdims=True)
        reading = picked[:, :dipoles] - picked[:, dipoles:]
        for i in range(dipoles // 128):
            read[pl.ds(s * (dipoles // 128) + i, 1)] = reading[:, i * 128:(i + 1) * 128]

    for s in range(sources):
        pick(s)

    def spread(devices, source, target, send, recv):
        copies = []
        for i, device in enumerate(devices):
            copies.append(pltpu.make_async_remote_copy(
                src_ref=source(i), dst_ref=target.at[i], send_sem=send.at[i], recv_sem=recv.at[i],
                device_id=device, device_id_type=MESH))
            copies[-1].start()
        return copies

    meet(3)
    read_copies = spread(others, lambda i: read, got, r_send, r_recv)

    sent(edge_field)
    sent(edge_adj)
    begin(edge_start)
    begin(edge_value)
    arrived(edge_field)

    def across(k, carry):
        for s in range(sources):
            ns[s, k] = ns[s, k] + (fe[s, k] + fe[s, k + 2])
        return carry

    lax.fori_loop(0, depth, across, 0)

    arrived(edge_adj)

    def adjoint_first(e, carry):
        for s in range(sources):
            center, total = around(e, ae, s, -1)
            a1[s, e] = KEEP * center + total
        return carry

    lax.fori_loop(0, depth + 4, adjoint_first, 0)

    def adjoint_second(e, carry):
        for s in range(sources):
            center, total = around(e, a1, s, 0)
            a2[s, e - 1] = KEEP * center + total
        return carry

    lax.fori_loop(1, depth + 3, adjoint_second, 0)

    for own, other, v in faces:
        lap[:, own] = lap[:, own] + (pe[own + 1] - pe[other + 1]).reshape(n_src, nx // n_src, ny)
    for k in range(depth - 1):
        face = (pe[k + 1] - pe[k + 2]).reshape(n_src, nx // n_src, ny)
        lap[:, k] = lap[:, k] + face
        lap[:, k + 1] = lap[:, k + 1] - face

    total = read[...]
    for i, copy in enumerate(read_copies):
        copy.wait_recv()
        total = total + got[i]
    for copy in read_copies:
        copy.wait_send()
    read[...] = total

    def scatter(s):
        per = dipoles // 128
        value = jnp.concatenate([read[pl.ds(s * per + i, 1)] for i in range(per)], axis=1) * weight_ref[pl.ds(s, 1)]
        value = jnp.concatenate([value, -value], axis=1)
        high = value.astype(jnp.bfloat16)
        low = (value - high.astype(jnp.float32)).astype(jnp.bfloat16)
        pieces = jnp.concatenate([spot[s, pl.ds(0, ny)] * high, spot[s, pl.ds(0, ny)] * low], axis=0)
        placed = lax.dot_general(hot[s], pieces, (((1,), (1,)), ((), ())), preferred_element_type=jnp.float32)
        placed = (placed[:, :ny] + placed[:, ny:]).reshape(depth + 4, nx, ny)
        b1[s] = ew[...] * placed

    for s in range(sources):
        scatter(s)

    def adjoint_readings(e, carry):
        for s in range(sources):
            center, total = around(e, b1, s, 0)
            a2[s, e - 1] = a2[s, e - 1] + (1.0 + KEEP) * center + total
        return carry

    lax.fori_loop(1, depth + 3, adjoint_readings, 0)

    def correlate(k, carry):
        product = empty
        mixed = empty
        for s in range(sources):
            adj, field = a2[s, k + 1], fe[s, k + 1]
            near_adj = a2[s, k] + a2[s, k + 2]
            for side in sides:
                near_adj = near_adj + neighbour(adj, side)
            product = product + adj * field
            mixed = mixed + (adj * ns[s, k] + field * near_adj)
            mixed = mixed - (a2[s, k] * fe[s, k] + a2[s, k + 2] * fe[s, k + 2])
        around_product = empty
        for side in sides:
            around_product = around_product + neighbour(product, side)
        result = (LEAKAGE + 3.0) * product + 0.5 * (around_product - mixed)
        co[:, k] = result.reshape(n_src, nx // n_src, ny)
        return carry

    lax.fori_loop(0, depth, correlate, 0)

    mate_copies = spread(mates, lambda i: co.at[mates[i][0]], rb, s_send, s_recv)

    arrived(edge_start)
    arrived(edge_value)
    for own, other, v in faces:
        sig_w, pert_w = face_weights(own, other)
        for s in range(sources):
            moved = pert_w * fe[s, other + 1]
            start = ie[s, other + 1]
            st[s, own + 1] = st[s, own + 1] + moved
            i1[s, own + 2] = i1[s, own + 2] + ew[own + 2] * (moved + sig_w * start)
            i1[s, other + 2] = i1[s, other + 2] + KEEP * start + ew[other + 2] * (vh[v, s] - moved)

    def increment(k, carry):
        for s in range(sources):
            center, total = around(k + 2, i1, s, 0)
            o2[s, k] = KEEP * center + ew[k + 2] * st[s, k + 1] + total
        return carry

    lax.fori_loop(0, depth, increment, 0)
    store = pltpu.make_async_copy(o2, inc_hbm, out_sem)
    store.start()

    total = co[src]
    for i, copy in enumerate(mate_copies):
        copy.wait_recv()
        total = total + rb[i]
    hess_ref[...] = REGULARIZE * lap[src] - total

    sent(edge_start)
    sent(edge_value)
    for copy in mate_copies:
        copy.wait_send()
    store.wait()


def on_device(conductivity, perturbation, fields, increment_start, adjoint_start, receivers, dipole_weight):
    sources, depth, nx, ny = fields.shape
    dipoles = dipole_weight.shape[1]
    n_src, n_gz = lax.axis_size("src"), lax.axis_size("gz")
    share = nx // n_src
    rows = sources * dipoles // 128

    def planes(*lead):
        return pltpu.VMEM((*lead, nx, ny), jnp.float32)

    others, mates = n_gz - 1, n_src - 1
    scratch = [
        pltpu.VMEM((sources, 2, dipoles), jnp.int32), pltpu.VMEM((sources, dipoles), jnp.float32),
        planes(depth + 6), planes(depth + 2), planes(sources, depth + 2), planes(sources, depth + 2),
        planes(sources, depth + 4), planes(sources, depth + 4), planes(sources, depth),
        planes(sources, depth + 6), planes(sources, depth + 4), planes(sources, depth + 2), planes(sources, depth + 4),
        planes(6, depth + 4), planes(depth + 4), planes(sources, depth), planes(sources, depth + 2),
        planes(2, sources), planes(sources, depth), pltpu.VMEM((n_src, depth, share, ny), jnp.float32),
        pltpu.VMEM((sources, (depth + 4) * nx, 2 * dipoles), jnp.bfloat16),
        pltpu.VMEM((sources, 3 * ny, 2 * dipoles), jnp.bfloat16),
        pltpu.VMEM((rows, 128), jnp.float32), pltpu.VMEM((others, rows, 128), jnp.float32),
        pltpu.VMEM((n_src, depth, share, ny), jnp.float32), pltpu.VMEM((mates, depth, share, ny), jnp.float32),
        DMA((7,)), DMA, pltpu.SemaphoreType.REGULAR((4,)), DMA((2, 6)), DMA((2, 6)), DMA((others,)), DMA((others,)),
        DMA((mates,)), DMA((mates,)),
    ]
    anywhere = pl.BlockSpec(memory_space=pltpu.HBM)
    vmem = pl.BlockSpec(memory_space=pltpu.VMEM)
    return pl.pallas_call(
        kernel,
        out_shape=(
            jax.ShapeDtypeStruct((depth, share, ny), jnp.float32),
            jax.ShapeDtypeStruct(increment_start.shape, jnp.float32),
        ),
        in_specs=[anywhere] * 7,
        out_specs=(vmem, anywhere),
        scratch_shapes=scratch,
        compiler_params=pltpu.CompilerParams(
            collective_id=0, has_side_effects=True, vmem_limit_bytes=63 * 2**20),
    )(conductivity, perturbation, fields, increment_start, adjoint_start, jnp.swapaxes(receivers, 1, 2), dipole_weight)


def solution(mesh):
    return jax.shard_map(
        on_device,
        mesh=mesh,
        in_specs=(
            P("gz", None, None),
            P("gz", None, None),
            P("src", "gz", None, None),
            P("src", "gz", None, None),
            P("src", "gz", None, None),
            P("src", None, None),
            P("src", None),
        ),
        out_specs=(P("gz", "src", None), P("src", "gz", None, None)),
        check_vma=False,
    )
```

```python
import functools

import jax
import jax.numpy as jnp
from jax import lax
from jax.experimental import pallas as pl
from jax.experimental.pallas import tpu as pltpu
from jax.sharding import PartitionSpec as P

LEAKAGE = 0.5
RELAXATION = 0.8
REGULARIZE = 0.05
KEEP = 1.0 - RELAXATION
MESH = pl.DeviceIdType.MESH
DMA = pltpu.SemaphoreType.DMA


def ahead(plane, axis):
    return pltpu.roll(plane, plane.shape[axis] - 1, axis)


def behind(plane, axis):
    return pltpu.roll(plane, 1, axis)


def kernel(
    sigma_hbm, pert_hbm, field_hbm, start_hbm, adjoint_hbm, cells_hbm, weight_hbm,
    hess_ref, inc_hbm,
    cells_ref, weight_ref, sg, pe, fe, ie, i1, i2, o2, ae, a1, a2, b1,
    coef, ew, nb, st, ih, ns, lap,
    hot, spot, read, got, co, rb,
    in_sem, out_sem, known, z_send, z_recv, c_send, c_recv, r_send, r_recv, s_send, s_recv,
):
    src, gz = lax.axis_index("src"), lax.axis_index("gz")
    n_src, n_gz = lax.axis_size("src"), lax.axis_size("gz")
    sources, depth, nx, ny = field_hbm.shape
    dipoles = weight_ref.shape[1]
    has_lo, has_hi = gz > 0, gz < n_gz - 1
    row = lax.broadcasted_iota(jnp.int32, (nx, ny), 0)
    col = lax.broadcasted_iota(jnp.int32, (nx, ny), 1)
    inside = {(0, 1): row < nx - 1, (0, -1): row > 0, (1, 1): col < ny - 1, (1, -1): col > 0}
    sides = tuple(inside)

    def shifted(plane, side):
        return ahead(plane, side[0]) if side[1] > 0 else behind(plane, side[0])

    def neighbour(plane, side):
        return jnp.where(inside[side], shifted(plane, side), 0.0)

    lo, hi = (src, gz - 1), (src, gz + 1)
    half = n_gz // 2
    x_part, z_part = gz // half, lax.rem(gz, half)

    def at(dx, dz):
        return (src, lax.rem(x_part + dx, 2) * half + lax.rem(z_part + dz + half, half))

    steps = sorted(range(half), key=lambda dz: -min(dz, half - dz))
    others = [at(dx, dz) for dz in steps for dx in (1, 0) if dx or dz]
    core = lax.rem(src, 2)
    sibling = (src + 1 - 2 * core, gz)
    mates = []
    for d in range(n_src // 2 - 1, -1, -1):
        pair = lax.rem(src // 2 + d, n_src // 2) * 2
        mates += [(pair + 1 - core, gz), (pair + core, gz)] if d else [sibling]

    barrier = pltpu.get_barrier_semaphore()

    def signal(device, semaphore=barrier):
        pl.semaphore_signal(semaphore, inc=1, device_id=device, device_id_type=MESH)

    greeted = [at(0, 1), at(0, -1), at(1, 0), *mates]
    joint = jnp.logical_or(gz == half - 1, gz == half)
    for device in greeted:
        signal(device)
    pl.when(joint)(lambda: signal((src, n_gz - 1 - gz)))

    rounds = [[at(0, 1), at(0, -1)], [at(0, 2), at(0, -2)], [at(0, 4), at(0, -4)], [at(1, 0)]]

    def tell(i):
        for device in rounds[i]:
            signal(device, known.at[i])

    def meet(i):
        pl.semaphore_wait(known.at[i], len(rounds[i]))

    loads = [
        pltpu.make_async_copy(sigma_hbm, sg.at[pl.ds(3, depth)], in_sem.at[0]),
        pltpu.make_async_copy(pert_hbm, pe.at[pl.ds(1, depth)], in_sem.at[1]),
        pltpu.make_async_copy(start_hbm, ie.at[:, pl.ds(1, depth)], in_sem.at[2]),
        pltpu.make_async_copy(field_hbm, fe.at[:, pl.ds(1, depth)], in_sem.at[3]),
        pltpu.make_async_copy(adjoint_hbm, ae.at[:, pl.ds(3, depth)], in_sem.at[4]),
        pltpu.make_async_copy(cells_hbm, cells_ref, in_sem.at[5]),
        pltpu.make_async_copy(weight_hbm, weight_ref, in_sem.at[6]),
    ]
    for load in loads:
        load.start()

    empty = jnp.zeros((nx, ny), jnp.float32)

    def clear(high):
        for i in range(3):
            sg[depth + 3 + i if high else i] = empty
            for s in range(sources):
                ae[s, depth + 3 + i if high else i] = empty
        e = depth + 1 if high else 0
        pe[e] = empty
        for s in range(sources):
            fe[s, e] = empty
            for i in range(2):
                ih[1 if high else 0, s, i] = empty

    pl.when(jnp.logical_not(has_lo))(lambda: clear(False))
    pl.when(jnp.logical_not(has_hi))(lambda: clear(True))

    def edge(index, up_src, up_dst, down_src, down_dst):
        up = pltpu.make_async_remote_copy(
            src_ref=up_src, dst_ref=up_dst, send_sem=z_send.at[0, index], recv_sem=z_recv.at[0, index],
            device_id=hi, device_id_type=MESH)
        down = pltpu.make_async_remote_copy(
            src_ref=down_src, dst_ref=down_dst, send_sem=z_send.at[1, index], recv_sem=z_recv.at[1, index],
            device_id=lo, device_id_type=MESH)
        return up, down

    def begin(pair):
        pl.when(has_hi)(pair[0].start)
        pl.when(has_lo)(pair[1].start)

    def sent(pair):
        pl.when(has_hi)(pair[0].wait_send)
        pl.when(has_lo)(pair[1].wait_send)

    def arrived(pair):
        pl.when(has_lo)(pair[0].wait_recv)
        pl.when(has_hi)(pair[1].wait_recv)

    rows_here = pl.ds(pl.multiple_of(core * (nx // 2), nx // 2), nx // 2)
    low_sigma, high_sigma = sg.at[pl.ds(0, 3), rows_here], sg.at[pl.ds(depth + 3, 3), rows_here]
    low_pert, high_pert = pe.at[0, rows_here], pe.at[depth + 1, rows_here]
    edge_sigma = edge(0, sigma_hbm.at[pl.ds(depth - 3, 3), rows_here], low_sigma,
                      sigma_hbm.at[pl.ds(0, 3), rows_here], high_sigma)
    edge_pert = edge(1, pert_hbm.at[depth - 1, rows_here], low_pert, pert_hbm.at[0, rows_here], high_pert)
    hands = []
    for i, half_planes in enumerate((low_sigma, low_pert, high_sigma, high_pert)):
        hands.append(pltpu.make_async_remote_copy(
            src_ref=half_planes, dst_ref=half_planes, send_sem=c_send.at[i], recv_sem=c_recv.at[i],
            device_id=sibling, device_id_type=MESH))
    edge_field = edge(2, field_hbm.at[:, depth - 1], fe.at[:, 0], field_hbm.at[:, 0], fe.at[:, depth + 1])
    edge_adj = edge(3, adjoint_hbm.at[:, pl.ds(depth - 3, 3)], ae.at[:, pl.ds(0, 3)],
                    adjoint_hbm.at[:, pl.ds(0, 3)], ae.at[:, pl.ds(depth + 3, 3)])
    edge_inc = edge(4, i2.at[:, pl.ds(depth + 2, 2)], ih.at[0], i2.at[:, pl.ds(0, 2)], ih.at[1])

    pl.semaphore_wait(barrier, len(greeted) + joint.astype(jnp.int32))

    begin(edge_sigma)
    begin(edge_pert)
    begin(edge_field)
    begin(edge_adj)
    tell(0)

    for load in loads:
        load.wait()

    def local(k, carry):
        below, above = jnp.maximum(k - 1, 0), jnp.minimum(k + 1, depth - 1)
        has_below, has_above = (k > 0).astype(jnp.float32), (k < depth - 1).astype(jnp.float32)
        sig, pert = sg[k + 3], pe[k + 1]
        sig_z = [has_below * 0.5 * (sig + sg[below + 3]), has_above * 0.5 * (sig + sg[above + 3])]
        pert_z = [has_below * 0.5 * (pert + pe[below + 1]), has_above * 0.5 * (pert + pe[above + 1])]
        near_pert = [neighbour(pert, side) for side in sides]
        sig_w = [jnp.where(inside[side], 0.5 * (sig + shifted(sig, side)), 0.0) for side in sides]
        pert_w = [jnp.where(inside[side], 0.5 * (pert + other), 0.0) for side, other in zip(sides, near_pert)]
        pert_sum = (near_pert[0] + near_pert[1]) + (near_pert[2] + near_pert[3])
        diag = LEAKAGE * pert + 2.0 * pert + 0.5 * pert_sum + pert_z[0] + pert_z[1]
        for s in range(sources):
            field, start = fe[s, k + 1], ie[s, k + 1]
            term = pert_z[0] * fe[s, below + 1] + pert_z[1] * fe[s, above + 1] - diag * field
            near_field = empty
            for side, weight in zip(sides, pert_w):
                other = neighbour(field, side)
                term = term + weight * other
                near_field = near_field + other
            st[s, k + 1] = term
            ns[s, k] = near_field
            total = term + sig_z[0] * ie[s, below + 1] + sig_z[1] * ie[s, above + 1]
            for side, weight in zip(sides, sig_w):
                total = total + weight * shifted(start, side)
            nb[s, k] = total
        lap[:, k] = (4.0 * pert - pert_sum).reshape(n_src, nx // n_src, ny)
        return carry

    lax.fori_loop(0, depth, local, 0)
    meet(0)
    tell(1)

    def electrodes(s):
        both = cells_ref[s]
        flat = jnp.concatenate([both[0:1], both[1:2]], axis=1)
        plane_row = flat // ny
        return plane_row - (gz * depth - 2) * nx, flat - plane_row * ny

    def mark(s):
        rows, columns = electrodes(s)
        spot_s = jnp.broadcast_to(columns, (ny, 2 * dipoles)) == lax.broadcasted_iota(jnp.int32, (ny, 2 * dipoles), 0)
        spot_s = jnp.where(spot_s, 1.0, 0.0).astype(jnp.bfloat16)
        for piece in range(3):
            spot[s, pl.ds(piece * ny, ny)] = spot_s

        def chunk(c, carry):
            index = lax.broadcasted_iota(jnp.int32, (nx, 2 * dipoles), 0) + c * nx
            match = jnp.broadcast_to(rows, (nx, 2 * dipoles)) == index
            hot[s, pl.ds(pl.multiple_of(c * nx, nx), nx)] = jnp.where(match, 1.0, 0.0).astype(jnp.bfloat16)
            return carry

        lax.fori_loop(0, depth + 4, chunk, 0)

    for s in range(sources):
        mark(s)
    meet(1)
    tell(2)

    def hand_on(side):
        edge_sigma[side].wait_recv()
        hands[2 * side].start()
        edge_pert[side].wait_recv()
        hands[2 * side + 1].start()

    def handed(side):
        for hand in hands[2 * side:2 * side + 2]:
            hand.wait()

    pl.when(has_lo)(lambda: hand_on(0))
    pl.when(has_hi)(lambda: hand_on(1))
    meet(2)
    tell(3)
    pl.when(has_lo)(lambda: handed(0))
    pl.when(has_hi)(lambda: handed(1))

    def coefficients(e, carry):
        sig, below, above = sg[e + 1], sg[e], sg[e + 2]
        others = [neighbour(sig, side) for side in sides]
        diag = (LEAKAGE + 3.0) * sig + 0.5 * (((others[0] + others[1]) + (others[2] + others[3])) + (below + above))
        plane = gz * depth + e - 2
        exists = jnp.logical_and(plane >= 0, plane < n_gz * depth)
        scale = jnp.where(exists, RELAXATION / diag, 0.0)
        ew[e] = scale
        scale = 0.5 * scale
        for i, side in enumerate(sides):
            coef[i, e] = jnp.where(inside[side], scale * (sig + others[i]), 0.0)
        coef[4, e] = scale * (sig + below)
        coef[5, e] = scale * (sig + above)
        return carry

    lax.fori_loop(0, depth + 4, coefficients, 0)

    def around(e, values, s, offset):
        v = e - offset
        center = values[s, v]
        total = coef[4, e] * values[s, v - 1] + coef[5, e] * values[s, v + 1]
        for i, side in enumerate(sides):
            total = total + coef[i, e] * shifted(center, side)
        return center, total

    faces = ((0, -1), (depth - 1, depth))

    def face_weights(own, other):
        return 0.5 * (sg[own + 3] + sg[other + 3]), 0.5 * (pe[own + 1] + pe[other + 1])

    for k in range(1, depth - 1):
        for s in range(sources):
            i1[s, k + 2] = KEEP * ie[s, k + 1] + ew[k + 2] * nb[s, k]
    for own, other in faces:
        sig_w, pert_w = face_weights(own, other)
        for s in range(sources):
            moved = pert_w * fe[s, own + 1]
            st[s, own + 1] = st[s, own + 1] - moved
            st[s, other + 1] = moved
            i1[s, own + 2] = KEEP * ie[s, own + 1] + ew[own + 2] * (nb[s, own] - moved)
            i1[s, other + 2] = ew[other + 2] * (sig_w * ie[s, own + 1] + moved)
    for s in range(sources):
        i1[s, 0] = empty
        i1[s, depth + 3] = empty

    def second(e, carry):
        for s in range(sources):
            center, total = around(e, i1, s, 0)
            i2[s, e] = KEEP * center + ew[e] * st[s, e - 1] + total
        return carry

    lax.fori_loop(1, depth + 3, second, 0)
    for s in range(sources):
        i2[s, 0] = coef[5, 0] * i1[s, 1]
        i2[s, depth + 3] = coef[4, depth + 3] * i1[s, depth + 2]

    def pick(s):
        rows, _ = electrodes(s)
        value = i2[s].reshape((depth + 4) * nx, ny)
        high = value.astype(jnp.bfloat16)
        rest = value - high.astype(jnp.float32)
        middle = rest.astype(jnp.bfloat16)
        low = (rest - middle.astype(jnp.float32)).astype(jnp.bfloat16)
        columns = jnp.dot(
            jnp.concatenate([high, middle, low], axis=1), spot[s], preferred_element_type=jnp.float32)
        index = lax.broadcasted_iota(jnp.int32, columns.shape, 0)
        picked = jnp.sum(jnp.where(jnp.broadcast_to(rows, columns.shape) == index, columns, 0.0), axis=0, keepdims=True)
        reading = picked[:, :dipoles] - picked[:, dipoles:]
        for i in range(dipoles // 128):
            read[pl.ds(s * (dipoles // 128) + i, 1)] = reading[:, i * 128:(i + 1) * 128]

    for s in range(sources):
        pick(s)

    def spread(devices, source, target, send, recv):
        copies = []
        for i, device in enumerate(devices):
            copies.append(pltpu.make_async_remote_copy(
                src_ref=source(i), dst_ref=target.at[i], send_sem=send.at[i], recv_sem=recv.at[i],
                device_id=device, device_id_type=MESH))
            copies[-1].start()
        return copies

    meet(3)
    read_copies = spread(others, lambda i: read, got, r_send, r_recv)

    sent(edge_sigma)
    sent(edge_pert)
    sent(edge_field)
    sent(edge_adj)
    arrived(edge_field)

    def across(k, carry):
        for s in range(sources):
            ns[s, k] = ns[s, k] + (fe[s, k] + fe[s, k + 2])
        return carry

    lax.fori_loop(0, depth, across, 0)

    arrived(edge_adj)
    begin(edge_inc)

    def adjoint_first(e, carry):
        for s in range(sources):
            center, total = around(e, ae, s, -1)
            a1[s, e] = KEEP * center + total
        return carry

    lax.fori_loop(0, depth + 4, adjoint_first, 0)

    def adjoint_second(e, carry):
        for s in range(sources):
            center, total = around(e, a1, s, 0)
            a2[s, e - 1] = KEEP * center + total
        return carry

    lax.fori_loop(1, depth + 3, adjoint_second, 0)

    for own, other in faces:
        lap[:, own] = lap[:, own] + (pe[own + 1] - pe[other + 1]).reshape(n_src, nx // n_src, ny)
    for k in range(depth - 1):
        face = (pe[k + 1] - pe[k + 2]).reshape(n_src, nx // n_src, ny)
        lap[:, k] = lap[:, k] + face
        lap[:, k + 1] = lap[:, k + 1] - face

    total = read[...]
    for i, copy in enumerate(read_copies):
        copy.wait_recv()
        total = total + got[i]
    for copy in read_copies:
        copy.wait_send()
    read[...] = total

    def scatter(s):
        per = dipoles // 128
        value = jnp.concatenate([read[pl.ds(s * per + i, 1)] for i in range(per)], axis=1) * weight_ref[pl.ds(s, 1)]
        value = jnp.concatenate([value, -value], axis=1)
        high = value.astype(jnp.bfloat16)
        low = (value - high.astype(jnp.float32)).astype(jnp.bfloat16)
        pieces = jnp.concatenate([spot[s, pl.ds(0, ny)] * high, spot[s, pl.ds(0, ny)] * low], axis=0)
        placed = lax.dot_general(hot[s], pieces, (((1,), (1,)), ((), ())), preferred_element_type=jnp.float32)
        placed = (placed[:, :ny] + placed[:, ny:]).reshape(depth + 4, nx, ny)
        b1[s] = ew[...] * placed

    for s in range(sources):
        scatter(s)

    def adjoint_readings(e, carry):
        for s in range(sources):
            center, total = around(e, b1, s, 0)
            a2[s, e - 1] = a2[s, e - 1] + (1.0 + KEEP) * center + total
        return carry

    lax.fori_loop(1, depth + 3, adjoint_readings, 0)

    def correlate(k, carry):
        product = empty
        mixed = empty
        for s in range(sources):
            adj, field = a2[s, k + 1], fe[s, k + 1]
            near_adj = a2[s, k] + a2[s, k + 2]
            for side in sides:
                near_adj = near_adj + neighbour(adj, side)
            product = product + adj * field
            mixed = mixed + (adj * ns[s, k] + field * near_adj)
            mixed = mixed - (a2[s, k] * fe[s, k] + a2[s, k + 2] * fe[s, k + 2])
        around_product = empty
        for side in sides:
            around_product = around_product + neighbour(product, side)
        result = (LEAKAGE + 3.0) * product + 0.5 * (around_product - mixed)
        co[:, k] = result.reshape(n_src, nx // n_src, ny)
        return carry

    lax.fori_loop(0, depth, correlate, 0)

    mate_copies = spread(mates, lambda i: co.at[mates[i][0]], rb, s_send, s_recv)

    arrived(edge_inc)
    for s in range(sources):
        for k in range(depth):
            o2[s, k] = i2[s, k + 2] + (ih[0, s, k] if k < 2 else ih[1, s, k + 2 - depth])
    store = pltpu.make_async_copy(o2, inc_hbm, out_sem)
    store.start()

    total = co[src]
    for i, copy in enumerate(mate_copies):
        copy.wait_recv()
        total = total + rb[i]
    hess_ref[...] = REGULARIZE * lap[src] - total

    sent(edge_inc)
    for copy in mate_copies:
        copy.wait_send()
    store.wait()


def on_device(conductivity, perturbation, fields, increment_start, adjoint_start, receivers, dipole_weight):
    sources, depth, nx, ny = fields.shape
    dipoles = dipole_weight.shape[1]
    n_src, n_gz = lax.axis_size("src"), lax.axis_size("gz")
    share = nx // n_src
    rows = sources * dipoles // 128

    def planes(*lead):
        return pltpu.VMEM((*lead, nx, ny), jnp.float32)

    others, mates = n_gz - 1, n_src - 1
    scratch = [
        pltpu.VMEM((sources, 2, dipoles), jnp.int32), pltpu.VMEM((sources, dipoles), jnp.float32),
        planes(depth + 6), planes(depth + 2), planes(sources, depth + 2), planes(sources, depth + 2),
        planes(sources, depth + 4), planes(sources, depth + 4), planes(sources, depth),
        planes(sources, depth + 6), planes(sources, depth + 4), planes(sources, depth + 2), planes(sources, depth + 4),
        planes(6, depth + 4), planes(depth + 4), planes(sources, depth), planes(sources, depth + 2),
        planes(2, sources, 2), planes(sources, depth), pltpu.VMEM((n_src, depth, share, ny), jnp.float32),
        pltpu.VMEM((sources, (depth + 4) * nx, 2 * dipoles), jnp.bfloat16),
        pltpu.VMEM((sources, 3 * ny, 2 * dipoles), jnp.bfloat16),
        pltpu.VMEM((rows, 128), jnp.float32), pltpu.VMEM((others, rows, 128), jnp.float32),
        pltpu.VMEM((n_src, depth, share, ny), jnp.float32), pltpu.VMEM((mates, depth, share, ny), jnp.float32),
        DMA((7,)), DMA, pltpu.SemaphoreType.REGULAR((4,)), DMA((2, 5)), DMA((2, 5)), DMA((4,)), DMA((4,)), DMA((others,)), DMA((others,)),
        DMA((mates,)), DMA((mates,)),
    ]
    anywhere = pl.BlockSpec(memory_space=pltpu.HBM)
    vmem = pl.BlockSpec(memory_space=pltpu.VMEM)
    return pl.pallas_call(
        kernel,
        out_shape=(
            jax.ShapeDtypeStruct((depth, share, ny), jnp.float32),
            jax.ShapeDtypeStruct(increment_start.shape, jnp.float32),
        ),
        in_specs=[anywhere] * 7,
        out_specs=(vmem, anywhere),
        scratch_shapes=scratch,
        compiler_params=pltpu.CompilerParams(
            collective_id=0, has_side_effects=True, vmem_limit_bytes=63 * 2**20),
    )(conductivity, perturbation, fields, increment_start, adjoint_start, jnp.swapaxes(receivers, 1, 2), dipole_weight)


def solution(mesh):
    return jax.shard_map(
        on_device,
        mesh=mesh,
        in_specs=(
            P("gz", None, None),
            P("gz", None, None),
            P("src", "gz", None, None),
            P("src", "gz", None, None),
            P("src", "gz", None, None),
            P("src", None, None),
            P("src", None),
        ),
        out_specs=(P("gz", "src", None), P("src", "gz", None, None)),
        check_vma=False,
    )
```

```python
import functools

import jax
import jax.numpy as jnp
from jax import lax
from jax.experimental import pallas as pl
from jax.experimental.pallas import tpu as pltpu
from jax.sharding import PartitionSpec as P

LEAKAGE = 0.5
RELAXATION = 0.8
REGULARIZE = 0.05
KEEP = 1.0 - RELAXATION
MESH = pl.DeviceIdType.MESH
DMA = pltpu.SemaphoreType.DMA


def ahead(plane, axis):
    return pltpu.roll(plane, plane.shape[axis] - 1, axis)


def behind(plane, axis):
    return pltpu.roll(plane, 1, axis)


def kernel(
    sigma_hbm, pert_hbm, field_hbm, start_hbm, adjoint_hbm, cells_hbm, weight_hbm,
    hess_ref, inc_hbm,
    cells_ref, weight_ref, sg, pe, fe, ie, i1, i2, o2, ae, a1, a2, b1,
    coef, ew, nb, st, ih, ns, lap,
    hot, spot, read, got, co, rb,
    in_sem, out_sem, known, z_send, z_recv, c_send, c_recv, r_send, r_recv, s_send, s_recv,
):
    src, gz = lax.axis_index("src"), lax.axis_index("gz")
    n_src, n_gz = lax.axis_size("src"), lax.axis_size("gz")
    sources, depth, nx, ny = field_hbm.shape
    dipoles = weight_ref.shape[1]
    has_lo, has_hi = gz > 0, gz < n_gz - 1
    row = lax.broadcasted_iota(jnp.int32, (nx, ny), 0)
    col = lax.broadcasted_iota(jnp.int32, (nx, ny), 1)
    inside = {(0, 1): row < nx - 1, (0, -1): row > 0, (1, 1): col < ny - 1, (1, -1): col > 0}
    sides = tuple(inside)

    def shifted(plane, side):
        return ahead(plane, side[0]) if side[1] > 0 else behind(plane, side[0])

    def neighbour(plane, side):
        return jnp.where(inside[side], shifted(plane, side), 0.0)

    lo, hi = (src, gz - 1), (src, gz + 1)
    half = n_gz // 2
    x_part, z_part = gz // half, lax.rem(gz, half)

    def at(dx, dz):
        return (src, lax.rem(x_part + dx, 2) * half + lax.rem(z_part + dz + half, half))

    steps = sorted(range(half), key=lambda dz: -min(dz, half - dz))
    others = [at(dx, dz) for dz in steps for dx in (1, 0) if dx or dz]
    core = lax.rem(src, 2)
    sibling = (src + 1 - 2 * core, gz)
    mates = []
    for d in range(n_src // 2 - 1, -1, -1):
        pair = lax.rem(src // 2 + d, n_src // 2) * 2
        mates += [(pair + 1 - core, gz), (pair + core, gz)] if d else [sibling]

    barrier = pltpu.get_barrier_semaphore()

    def signal(device, semaphore=barrier):
        pl.semaphore_signal(semaphore, inc=1, device_id=device, device_id_type=MESH)

    greeted = [at(0, 1), at(0, -1), at(1, 0), *mates]
    joint = jnp.logical_or(gz == half - 1, gz == half)
    for device in greeted:
        signal(device)
    pl.when(joint)(lambda: signal((src, n_gz - 1 - gz)))

    rounds = [[at(0, 1), at(0, -1)], [at(0, 2), at(0, -2)], [at(0, 4), at(0, -4)], [at(1, 0)]]

    def tell(i):
        for device in rounds[i]:
            signal(device, known.at[i])

    def meet(i):
        pl.semaphore_wait(known.at[i], len(rounds[i]))

    loads = [
        pltpu.make_async_copy(sigma_hbm, sg.at[pl.ds(3, depth)], in_sem.at[0]),
        pltpu.make_async_copy(pert_hbm, pe.at[pl.ds(1, depth)], in_sem.at[1]),
        pltpu.make_async_copy(start_hbm, ie.at[:, pl.ds(1, depth)], in_sem.at[2]),
        pltpu.make_async_copy(field_hbm, fe.at[:, pl.ds(1, depth)], in_sem.at[3]),
        pltpu.make_async_copy(adjoint_hbm, ae.at[:, pl.ds(3, depth)], in_sem.at[4]),
        pltpu.make_async_copy(cells_hbm, cells_ref, in_sem.at[5]),
        pltpu.make_async_copy(weight_hbm, weight_ref, in_sem.at[6]),
    ]
    for load in loads:
        load.start()

    empty = jnp.zeros((nx, ny), jnp.float32)

    def clear(high):
        for i in range(3):
            sg[depth + 3 + i if high else i] = empty
            for s in range(sources):
                ae[s, depth + 3 + i if high else i] = empty
        e = depth + 1 if high else 0
        pe[e] = empty
        for s in range(sources):
            fe[s, e] = empty
            for i in range(2):
                ih[1 if high else 0, s, i] = empty

    pl.when(jnp.logical_not(has_lo))(lambda: clear(False))
    pl.when(jnp.logical_not(has_hi))(lambda: clear(True))

    def edge(index, up_src, up_dst, down_src, down_dst):
        up = pltpu.make_async_remote_copy(
            src_ref=up_src, dst_ref=up_dst, send_sem=z_send.at[0, index], recv_sem=z_recv.at[0, index],
            device_id=hi, device_id_type=MESH)
        down = pltpu.make_async_remote_copy(
            src_ref=down_src, dst_ref=down_dst, send_sem=z_send.at[1, index], recv_sem=z_recv.at[1, index],
            device_id=lo, device_id_type=MESH)
        return up, down

    def begin(pair):
        pl.when(has_hi)(pair[0].start)
        pl.when(has_lo)(pair[1].start)

    def sent(pair):
        pl.when(has_hi)(pair[0].wait_send)
        pl.when(has_lo)(pair[1].wait_send)

    def arrived(pair):
        pl.when(has_lo)(pair[0].wait_recv)
        pl.when(has_hi)(pair[1].wait_recv)

    rows_here = pl.ds(pl.multiple_of(core * (nx // 2), nx // 2), nx // 2)
    low_sigma, high_sigma = sg.at[pl.ds(0, 3), rows_here], sg.at[pl.ds(depth + 3, 3), rows_here]
    low_pert, high_pert = pe.at[0, rows_here], pe.at[depth + 1, rows_here]
    edge_sigma = edge(0, sigma_hbm.at[pl.ds(depth - 3, 3), rows_here], low_sigma,
                      sigma_hbm.at[pl.ds(0, 3), rows_here], high_sigma)
    edge_pert = edge(1, pert_hbm.at[depth - 1, rows_here], low_pert, pert_hbm.at[0, rows_here], high_pert)
    hands = []
    for i, half_planes in enumerate((low_sigma, low_pert, high_sigma, high_pert)):
        hands.append(pltpu.make_async_remote_copy(
            src_ref=half_planes, dst_ref=half_planes, send_sem=c_send.at[i], recv_sem=c_recv.at[i],
            device_id=sibling, device_id_type=MESH))
    edge_field = edge(2, field_hbm.at[:, depth - 1], fe.at[:, 0], field_hbm.at[:, 0], fe.at[:, depth + 1])
    edge_adj = edge(3, adjoint_hbm.at[:, pl.ds(depth - 3, 3)], ae.at[:, pl.ds(0, 3)],
                    adjoint_hbm.at[:, pl.ds(0, 3)], ae.at[:, pl.ds(depth + 3, 3)])
    edge_inc = edge(4, i2.at[:, pl.ds(depth + 2, 2)], ih.at[0], i2.at[:, pl.ds(0, 2)], ih.at[1])

    pl.semaphore_wait(barrier, len(greeted) + joint.astype(jnp.int32))

    begin(edge_sigma)
    begin(edge_pert)
    begin(edge_adj)
    begin(edge_field)
    tell(0)

    for load in loads:
        load.wait()

    def local(k, carry):
        below, above = jnp.maximum(k - 1, 0), jnp.minimum(k + 1, depth - 1)
        has_below, has_above = (k > 0).astype(jnp.float32), (k < depth - 1).astype(jnp.float32)
        sig, pert = sg[k + 3], pe[k + 1]
        sig_z = [has_below * 0.5 * (sig + sg[below + 3]), has_above * 0.5 * (sig + sg[above + 3])]
        pert_z = [has_below * 0.5 * (pert + pe[below + 1]), has_above * 0.5 * (pert + pe[above + 1])]
        near_pert = [neighbour(pert, side) for side in sides]
        sig_w = [jnp.where(inside[side], 0.5 * (sig + shifted(sig, side)), 0.0) for side in sides]
        pert_w = [jnp.where(inside[side], 0.5 * (pert + other), 0.0) for side, other in zip(sides, near_pert)]
        pert_sum = (near_pert[0] + near_pert[1]) + (near_pert[2] + near_pert[3])
        diag = LEAKAGE * pert + 2.0 * pert + 0.5 * pert_sum + pert_z[0] + pert_z[1]
        for s in range(sources):
            field, start = fe[s, k + 1], ie[s, k + 1]
            term = pert_z[0] * fe[s, below + 1] + pert_z[1] * fe[s, above + 1] - diag * field
            near_field = empty
            for side, weight in zip(sides, pert_w):
                other = neighbour(field, side)
                term = term + weight * other
                near_field = near_field + other
            st[s, k + 1] = term
            ns[s, k] = near_field
            total = term + sig_z[0] * ie[s, below + 1] + sig_z[1] * ie[s, above + 1]
            for side, weight in zip(sides, sig_w):
                total = total + weight * shifted(start, side)
            nb[s, k] = total
        lap[:, k] = (4.0 * pert - pert_sum).reshape(n_src, nx // n_src, ny)
        return carry

    lax.fori_loop(0, depth, local, 0)
    meet(0)
    tell(1)

    def electrodes(s):
        both = cells_ref[s]
        flat = jnp.concatenate([both[0:1], both[1:2]], axis=1)
        plane_row = flat // ny
        return plane_row - (gz * depth - 2) * nx, flat - plane_row * ny

    def mark(s):
        rows, columns = electrodes(s)
        spot_s = jnp.broadcast_to(columns, (ny, 2 * dipoles)) == lax.broadcasted_iota(jnp.int32, (ny, 2 * dipoles), 0)
        spot_s = jnp.where(spot_s, 1.0, 0.0).astype(jnp.bfloat16)
        for piece in range(3):
            spot[s, pl.ds(piece * ny, ny)] = spot_s

        def chunk(c, carry):
            index = lax.broadcasted_iota(jnp.int32, (nx, 2 * dipoles), 0) + c * nx
            match = jnp.broadcast_to(rows, (nx, 2 * dipoles)) == index
            hot[s, pl.ds(pl.multiple_of(c * nx, nx), nx)] = jnp.where(match, 1.0, 0.0).astype(jnp.bfloat16)
            return carry

        lax.fori_loop(0, depth + 4, chunk, 0)

    for s in range(sources):
        mark(s)
    meet(1)
    tell(2)

    def hand_on(side):
        edge_sigma[side].wait_recv()
        hands[2 * side].start()
        edge_pert[side].wait_recv()
        hands[2 * side + 1].start()

    def handed(side):
        for hand in hands[2 * side:2 * side + 2]:
            hand.wait()

    pl.when(has_lo)(lambda: hand_on(0))
    pl.when(has_hi)(lambda: hand_on(1))
    meet(2)
    tell(3)
    pl.when(has_lo)(lambda: handed(0))
    pl.when(has_hi)(lambda: handed(1))

    def coefficients(e, carry):
        sig, below, above = sg[e + 1], sg[e], sg[e + 2]
        others = [neighbour(sig, side) for side in sides]
        diag = (LEAKAGE + 3.0) * sig + 0.5 * (((others[0] + others[1]) + (others[2] + others[3])) + (below + above))
        plane = gz * depth + e - 2
        exists = jnp.logical_and(plane >= 0, plane < n_gz * depth)
        scale = jnp.where(exists, RELAXATION / diag, 0.0)
        ew[e] = scale
        scale = 0.5 * scale
        for i, side in enumerate(sides):
            coef[i, e] = jnp.where(inside[side], scale * (sig + others[i]), 0.0)
        coef[4, e] = scale * (sig + below)
        coef[5, e] = scale * (sig + above)
        return carry

    lax.fori_loop(0, depth + 4, coefficients, 0)

    def around(e, values, s, offset):
        v = e - offset
        center = values[s, v]
        total = coef[4, e] * values[s, v - 1] + coef[5, e] * values[s, v + 1]
        for i, side in enumerate(sides):
            total = total + coef[i, e] * shifted(center, side)
        return center, total

    faces = ((0, -1), (depth - 1, depth))

    def face_weights(own, other):
        return 0.5 * (sg[own + 3] + sg[other + 3]), 0.5 * (pe[own + 1] + pe[other + 1])

    for k in range(1, depth - 1):
        for s in range(sources):
            i1[s, k + 2] = KEEP * ie[s, k + 1] + ew[k + 2] * nb[s, k]
    for own, other in faces:
        sig_w, pert_w = face_weights(own, other)
        for s in range(sources):
            moved = pert_w * fe[s, own + 1]
            st[s, own + 1] = st[s, own + 1] - moved
            st[s, other + 1] = moved
            i1[s, own + 2] = KEEP * ie[s, own + 1] + ew[own + 2] * (nb[s, own] - moved)
            i1[s, other + 2] = ew[other + 2] * (sig_w * ie[s, own + 1] + moved)
    for s in range(sources):
        i1[s, 0] = empty
        i1[s, depth + 3] = empty

    def second(e, carry):
        for s in range(sources):
            center, total = around(e, i1, s, 0)
            i2[s, e] = KEEP * center + ew[e] * st[s, e - 1] + total
        return carry

    lax.fori_loop(1, depth + 3, second, 0)
    for s in range(sources):
        i2[s, 0] = coef[5, 0] * i1[s, 1]
        i2[s, depth + 3] = coef[4, depth + 3] * i1[s, depth + 2]

    def pick(s):
        rows, _ = electrodes(s)
        value = i2[s].reshape((depth + 4) * nx, ny)
        high = value.astype(jnp.bfloat16)
        rest = value - high.astype(jnp.float32)
        middle = rest.astype(jnp.bfloat16)
        low = (rest - middle.astype(jnp.float32)).astype(jnp.bfloat16)
        columns = jnp.dot(
            jnp.concatenate([high, middle, low], axis=1), spot[s], preferred_element_type=jnp.float32)
        index = lax.broadcasted_iota(jnp.int32, columns.shape, 0)
        picked = jnp.sum(jnp.where(jnp.broadcast_to(rows, columns.shape) == index, columns, 0.0), axis=0, keepdims=True)
        reading = picked[:, :dipoles] - picked[:, dipoles:]
        for i in range(dipoles // 128):
            read[pl.ds(s * (dipoles // 128) + i, 1)] = reading[:, i * 128:(i + 1) * 128]

    for s in range(sources):
        pick(s)

    def spread(devices, source, target, send, recv):
        copies = []
        for i, device in enumerate(devices):
            copies.append(pltpu.make_async_remote_copy(
                src_ref=source(i), dst_ref=target.at[i], send_sem=send.at[i], recv_sem=recv.at[i],
                device_id=device, device_id_type=MESH))
            copies[-1].start()
        return copies

    meet(3)
    read_copies = spread(others, lambda i: read, got, r_send, r_recv)


    arrived(edge_adj)
    begin(edge_inc)

    def adjoint_first(e, carry):
        for s in range(sources):
            center, total = around(e, ae, s, -1)
            a1[s, e] = KEEP * center + total
        return carry

    lax.fori_loop(0, depth + 4, adjoint_first, 0)

    def adjoint_second(e, carry):
        for s in range(sources):
            center, total = around(e, a1, s, 0)
            a2[s, e - 1] = KEEP * center + total
        return carry

    lax.fori_loop(1, depth + 3, adjoint_second, 0)

    for own, other in faces:
        lap[:, own] = lap[:, own] + (pe[own + 1] - pe[other + 1]).reshape(n_src, nx // n_src, ny)
    for k in range(depth - 1):
        face = (pe[k + 1] - pe[k + 2]).reshape(n_src, nx // n_src, ny)
        lap[:, k] = lap[:, k] + face
        lap[:, k + 1] = lap[:, k + 1] - face

    total = read[...]
    for i, copy in enumerate(read_copies):
        copy.wait_recv()
        total = total + got[i]
    for copy in read_copies:
        copy.wait_send()
    read[...] = total

    def scatter(s):
        per = dipoles // 128
        value = jnp.concatenate([read[pl.ds(s * per + i, 1)] for i in range(per)], axis=1) * weight_ref[pl.ds(s, 1)]
        value = jnp.concatenate([value, -value], axis=1)
        high = value.astype(jnp.bfloat16)
        low = (value - high.astype(jnp.float32)).astype(jnp.bfloat16)
        pieces = jnp.concatenate([spot[s, pl.ds(0, ny)] * high, spot[s, pl.ds(0, ny)] * low], axis=0)
        placed = lax.dot_general(hot[s], pieces, (((1,), (1,)), ((), ())), preferred_element_type=jnp.float32)
        placed = (placed[:, :ny] + placed[:, ny:]).reshape(depth + 4, nx, ny)
        b1[s] = ew[...] * placed

    for s in range(sources):
        scatter(s)

    def adjoint_readings(e, carry):
        for s in range(sources):
            center, total = around(e, b1, s, 0)
            a2[s, e - 1] = a2[s, e - 1] + (1.0 + KEEP) * center + total
        return carry

    lax.fori_loop(1, depth + 3, adjoint_readings, 0)

    arrived(edge_field)

    def across(k, carry):
        for s in range(sources):
            ns[s, k] = ns[s, k] + (fe[s, k] + fe[s, k + 2])
        return carry

    lax.fori_loop(0, depth, across, 0)

    def correlate(k, carry):
        product = empty
        mixed = empty
        for s in range(sources):
            adj, field = a2[s, k + 1], fe[s, k + 1]
            near_adj = a2[s, k] + a2[s, k + 2]
            for side in sides:
                near_adj = near_adj + neighbour(adj, side)
            product = product + adj * field
            mixed = mixed + (adj * ns[s, k] + field * near_adj)
            mixed = mixed - (a2[s, k] * fe[s, k] + a2[s, k + 2] * fe[s, k + 2])
        around_product = empty
        for side in sides:
            around_product = around_product + neighbour(product, side)
        result = (LEAKAGE + 3.0) * product + 0.5 * (around_product - mixed)
        co[:, k] = result.reshape(n_src, nx // n_src, ny)
        return carry

    lax.fori_loop(0, depth, correlate, 0)

    mate_copies = spread(mates, lambda i: co.at[mates[i][0]], rb, s_send, s_recv)

    arrived(edge_inc)
    for s in range(sources):
        for k in range(depth):
            o2[s, k] = i2[s, k + 2] + (ih[0, s, k] if k < 2 else ih[1, s, k + 2 - depth])
    store = pltpu.make_async_copy(o2, inc_hbm, out_sem)
    store.start()

    total = co[src]
    for i, copy in enumerate(mate_copies):
        copy.wait_recv()
        total = total + rb[i]
    hess_ref[...] = REGULARIZE * lap[src] - total

    for pair in (edge_sigma, edge_pert, edge_adj, edge_field, edge_inc):
        sent(pair)
    for copy in mate_copies:
        copy.wait_send()
    store.wait()


def on_device(conductivity, perturbation, fields, increment_start, adjoint_start, receivers, dipole_weight):
    sources, depth, nx, ny = fields.shape
    dipoles = dipole_weight.shape[1]
    n_src, n_gz = lax.axis_size("src"), lax.axis_size("gz")
    share = nx // n_src
    rows = sources * dipoles // 128

    def planes(*lead):
        return pltpu.VMEM((*lead, nx, ny), jnp.float32)

    others, mates = n_gz - 1, n_src - 1
    scratch = [
        pltpu.VMEM((sources, 2, dipoles), jnp.int32), pltpu.VMEM((sources, dipoles), jnp.float32),
        planes(depth + 6), planes(depth + 2), planes(sources, depth + 2), planes(sources, depth + 2),
        planes(sources, depth + 4), planes(sources, depth + 4), planes(sources, depth),
        planes(sources, depth + 6), planes(sources, depth + 4), planes(sources, depth + 2), planes(sources, depth + 4),
        planes(6, depth + 4), planes(depth + 4), planes(sources, depth), planes(sources, depth + 2),
        planes(2, sources, 2), planes(sources, depth), pltpu.VMEM((n_src, depth, share, ny), jnp.float32),
        pltpu.VMEM((sources, (depth + 4) * nx, 2 * dipoles), jnp.bfloat16),
        pltpu.VMEM((sources, 3 * ny, 2 * dipoles), jnp.bfloat16),
        pltpu.VMEM((rows, 128), jnp.float32), pltpu.VMEM((others, rows, 128), jnp.float32),
        pltpu.VMEM((n_src, depth, share, ny), jnp.float32), pltpu.VMEM((mates, depth, share, ny), jnp.float32),
        DMA((7,)), DMA, pltpu.SemaphoreType.REGULAR((4,)), DMA((2, 5)), DMA((2, 5)), DMA((4,)), DMA((4,)), DMA((others,)), DMA((others,)),
        DMA((mates,)), DMA((mates,)),
    ]
    anywhere = pl.BlockSpec(memory_space=pltpu.HBM)
    vmem = pl.BlockSpec(memory_space=pltpu.VMEM)
    return pl.pallas_call(
        kernel,
        out_shape=(
            jax.ShapeDtypeStruct((depth, share, ny), jnp.float32),
            jax.ShapeDtypeStruct(increment_start.shape, jnp.float32),
        ),
        in_specs=[anywhere] * 7,
        out_specs=(vmem, anywhere),
        scratch_shapes=scratch,
        compiler_params=pltpu.CompilerParams(
            collective_id=0, has_side_effects=True, vmem_limit_bytes=63 * 2**20),
    )(conductivity, perturbation, fields, increment_start, adjoint_start, jnp.swapaxes(receivers, 1, 2), dipole_weight)


def solution(mesh):
    return jax.shard_map(
        on_device,
        mesh=mesh,
        in_specs=(
            P("gz", None, None),
            P("gz", None, None),
            P("src", "gz", None, None),
            P("src", "gz", None, None),
            P("src", "gz", None, None),
            P("src", None, None),
            P("src", None),
        ),
        out_specs=(P("gz", "src", None), P("src", "gz", None, None)),
        check_vma=False,
    )
```

```python
import functools

import jax
import jax.numpy as jnp
from jax import lax
from jax.experimental import pallas as pl
from jax.experimental.pallas import tpu as pltpu
from jax.sharding import PartitionSpec as P

LEAKAGE = 0.5
RELAXATION = 0.8
REGULARIZE = 0.05
KEEP = 1.0 - RELAXATION
MESH = pl.DeviceIdType.MESH
DMA = pltpu.SemaphoreType.DMA


def ahead(plane, axis):
    return pltpu.roll(plane, plane.shape[axis] - 1, axis)


def behind(plane, axis):
    return pltpu.roll(plane, 1, axis)


def kernel(
    sigma_hbm, pert_hbm, field_hbm, start_hbm, adjoint_hbm, cells_hbm, weight_hbm,
    hess_ref, inc_hbm,
    cells_ref, weight_ref, sg, pe, fe, ie, i1, i2, o2, ae, a1, a2, b1,
    coef, ew, nb, st, ih, ns, lap,
    hot, spot, read, got_pair, part, got, co, rb,
    in_sem, out_sem, known, z_send, z_recv, c_send, c_recv, p_send, p_recv, r_send, r_recv, s_send, s_recv,
):
    src, gz = lax.axis_index("src"), lax.axis_index("gz")
    n_src, n_gz = lax.axis_size("src"), lax.axis_size("gz")
    sources, depth, nx, ny = field_hbm.shape
    dipoles = weight_ref.shape[1]
    has_lo, has_hi = gz > 0, gz < n_gz - 1
    row = lax.broadcasted_iota(jnp.int32, (nx, ny), 0)
    col = lax.broadcasted_iota(jnp.int32, (nx, ny), 1)
    inside = {(0, 1): row < nx - 1, (0, -1): row > 0, (1, 1): col < ny - 1, (1, -1): col > 0}
    sides = tuple(inside)

    def shifted(plane, side):
        return ahead(plane, side[0]) if side[1] > 0 else behind(plane, side[0])

    def neighbour(plane, side):
        return jnp.where(inside[side], shifted(plane, side), 0.0)

    lo, hi = (src, gz - 1), (src, gz + 1)
    half = n_gz // 2
    x_part, z_part = gz // half, lax.rem(gz, half)

    def at(dx, dz):
        return (src, lax.rem(x_part + dx, 2) * half + lax.rem(z_part + dz + half, half))

    steps = sorted(range(half), key=lambda dz: -min(dz, half - dz))
    ring = [at(0, dz) for dz in steps if dz]
    core = lax.rem(src, 2)
    sibling = (src + 1 - 2 * core, gz)
    mates = []
    for d in range(n_src // 2 - 1, -1, -1):
        pair = lax.rem(src // 2 + d, n_src // 2) * 2
        mates += [(pair + 1 - core, gz), (pair + core, gz)] if d else [sibling]

    barrier = pltpu.get_barrier_semaphore()

    def signal(device, semaphore=barrier):
        pl.semaphore_signal(semaphore, inc=1, device_id=device, device_id_type=MESH)

    greeted = [at(0, 1), at(0, -1), at(1, 0), *mates]
    joint = jnp.logical_or(gz == half - 1, gz == half)
    for device in greeted:
        signal(device)
    pl.when(joint)(lambda: signal((src, n_gz - 1 - gz)))

    rounds = [[at(0, 1), at(0, -1)], [at(0, 2), at(0, -2)], [at(0, 4), at(0, -4)]]

    def tell(i):
        for device in rounds[i]:
            signal(device, known.at[i])

    def meet(i):
        pl.semaphore_wait(known.at[i], len(rounds[i]))

    loads = [
        pltpu.make_async_copy(sigma_hbm, sg.at[pl.ds(3, depth)], in_sem.at[0]),
        pltpu.make_async_copy(pert_hbm, pe.at[pl.ds(1, depth)], in_sem.at[1]),
        pltpu.make_async_copy(start_hbm, ie.at[:, pl.ds(1, depth)], in_sem.at[2]),
        pltpu.make_async_copy(field_hbm, fe.at[:, pl.ds(1, depth)], in_sem.at[3]),
        pltpu.make_async_copy(adjoint_hbm, ae.at[:, pl.ds(3, depth)], in_sem.at[4]),
        pltpu.make_async_copy(cells_hbm, cells_ref, in_sem.at[5]),
        pltpu.make_async_copy(weight_hbm, weight_ref, in_sem.at[6]),
    ]
    for load in loads:
        load.start()

    empty = jnp.zeros((nx, ny), jnp.float32)

    def clear(high):
        for i in range(3):
            sg[depth + 3 + i if high else i] = empty
            for s in range(sources):
                ae[s, depth + 3 + i if high else i] = empty
        e = depth + 1 if high else 0
        pe[e] = empty
        for s in range(sources):
            fe[s, e] = empty
            for i in range(2):
                ih[1 if high else 0, s, i] = empty

    pl.when(jnp.logical_not(has_lo))(lambda: clear(False))
    pl.when(jnp.logical_not(has_hi))(lambda: clear(True))

    def edge(index, up_src, up_dst, down_src, down_dst):
        up = pltpu.make_async_remote_copy(
            src_ref=up_src, dst_ref=up_dst, send_sem=z_send.at[0, index], recv_sem=z_recv.at[0, index],
            device_id=hi, device_id_type=MESH)
        down = pltpu.make_async_remote_copy(
            src_ref=down_src, dst_ref=down_dst, send_sem=z_send.at[1, index], recv_sem=z_recv.at[1, index],
            device_id=lo, device_id_type=MESH)
        return up, down

    def begin(pair):
        pl.when(has_hi)(pair[0].start)
        pl.when(has_lo)(pair[1].start)

    def sent(pair):
        pl.when(has_hi)(pair[0].wait_send)
        pl.when(has_lo)(pair[1].wait_send)

    def arrived(pair):
        pl.when(has_lo)(pair[0].wait_recv)
        pl.when(has_hi)(pair[1].wait_recv)

    rows_here = pl.ds(pl.multiple_of(core * (nx // 2), nx // 2), nx // 2)
    low_sigma, high_sigma = sg.at[pl.ds(0, 3), rows_here], sg.at[pl.ds(depth + 3, 3), rows_here]
    low_pert, high_pert = pe.at[0, rows_here], pe.at[depth + 1, rows_here]
    edge_sigma = edge(0, sigma_hbm.at[pl.ds(depth - 3, 3), rows_here], low_sigma,
                      sigma_hbm.at[pl.ds(0, 3), rows_here], high_sigma)
    edge_pert = edge(1, pert_hbm.at[depth - 1, rows_here], low_pert, pert_hbm.at[0, rows_here], high_pert)
    hands = []
    for i, half_planes in enumerate((low_sigma, low_pert, high_sigma, high_pert)):
        hands.append(pltpu.make_async_remote_copy(
            src_ref=half_planes, dst_ref=half_planes, send_sem=c_send.at[i], recv_sem=c_recv.at[i],
            device_id=sibling, device_id_type=MESH))
    edge_field = edge(2, field_hbm.at[:, depth - 1], fe.at[:, 0], field_hbm.at[:, 0], fe.at[:, depth + 1])
    edge_adj = edge(3, adjoint_hbm.at[:, pl.ds(depth - 3, 3)], ae.at[:, pl.ds(0, 3)],
                    adjoint_hbm.at[:, pl.ds(0, 3)], ae.at[:, pl.ds(depth + 3, 3)])
    edge_inc = edge(4, i2.at[:, pl.ds(depth + 2, 2)], ih.at[0], i2.at[:, pl.ds(0, 2)], ih.at[1])

    pl.semaphore_wait(barrier, len(greeted) + joint.astype(jnp.int32))

    begin(edge_sigma)
    begin(edge_pert)
    begin(edge_adj)
    begin(edge_field)
    tell(0)

    for load in loads:
        load.wait()

    def local(k, carry):
        below, above = jnp.maximum(k - 1, 0), jnp.minimum(k + 1, depth - 1)
        has_below, has_above = (k > 0).astype(jnp.float32), (k < depth - 1).astype(jnp.float32)
        sig, pert = sg[k + 3], pe[k + 1]
        sig_z = [has_below * 0.5 * (sig + sg[below + 3]), has_above * 0.5 * (sig + sg[above + 3])]
        pert_z = [has_below * 0.5 * (pert + pe[below + 1]), has_above * 0.5 * (pert + pe[above + 1])]
        near_pert = [neighbour(pert, side) for side in sides]
        sig_w = [jnp.where(inside[side], 0.5 * (sig + shifted(sig, side)), 0.0) for side in sides]
        pert_w = [jnp.where(inside[side], 0.5 * (pert + other), 0.0) for side, other in zip(sides, near_pert)]
        pert_sum = (near_pert[0] + near_pert[1]) + (near_pert[2] + near_pert[3])
        diag = LEAKAGE * pert + 2.0 * pert + 0.5 * pert_sum + pert_z[0] + pert_z[1]
        for s in range(sources):
            field, start = fe[s, k + 1], ie[s, k + 1]
            term = pert_z[0] * fe[s, below + 1] + pert_z[1] * fe[s, above + 1] - diag * field
            near_field = empty
            for side, weight in zip(sides, pert_w):
                other = neighbour(field, side)
                term = term + weight * other
                near_field = near_field + other
            st[s, k + 1] = term
            ns[s, k] = near_field
            total = term + sig_z[0] * ie[s, below + 1] + sig_z[1] * ie[s, above + 1]
            for side, weight in zip(sides, sig_w):
                total = total + weight * shifted(start, side)
            nb[s, k] = total
        lap[:, k] = (4.0 * pert - pert_sum).reshape(n_src, nx // n_src, ny)
        return carry

    lax.fori_loop(0, depth, local, 0)
    meet(0)
    tell(1)

    def electrodes(s):
        both = cells_ref[s]
        flat = jnp.concatenate([both[0:1], both[1:2]], axis=1)
        plane_row = flat // ny
        return plane_row - (gz * depth - 2) * nx, flat - plane_row * ny

    def mark(s):
        rows, columns = electrodes(s)
        spot_s = jnp.broadcast_to(columns, (ny, 2 * dipoles)) == lax.broadcasted_iota(jnp.int32, (ny, 2 * dipoles), 0)
        spot_s = jnp.where(spot_s, 1.0, 0.0).astype(jnp.bfloat16)
        for piece in range(3):
            spot[s, pl.ds(piece * ny, ny)] = spot_s

        def chunk(c, carry):
            index = lax.broadcasted_iota(jnp.int32, (nx, 2 * dipoles), 0) + c * nx
            match = jnp.broadcast_to(rows, (nx, 2 * dipoles)) == index
            hot[s, pl.ds(pl.multiple_of(c * nx, nx), nx)] = jnp.where(match, 1.0, 0.0).astype(jnp.bfloat16)
            return carry

        lax.fori_loop(0, depth + 4, chunk, 0)

    for s in range(sources):
        mark(s)
    meet(1)
    tell(2)

    def hand_on(side):
        edge_sigma[side].wait_recv()
        hands[2 * side].start()
        edge_pert[side].wait_recv()
        hands[2 * side + 1].start()

    def handed(side):
        for hand in hands[2 * side:2 * side + 2]:
            hand.wait()

    pl.when(has_lo)(lambda: hand_on(0))
    pl.when(has_hi)(lambda: hand_on(1))
    meet(2)
    pl.when(has_lo)(lambda: handed(0))
    pl.when(has_hi)(lambda: handed(1))

    def coefficients(e, carry):
        sig, below, above = sg[e + 1], sg[e], sg[e + 2]
        others = [neighbour(sig, side) for side in sides]
        diag = (LEAKAGE + 3.0) * sig + 0.5 * (((others[0] + others[1]) + (others[2] + others[3])) + (below + above))
        plane = gz * depth + e - 2
        exists = jnp.logical_and(plane >= 0, plane < n_gz * depth)
        scale = jnp.where(exists, RELAXATION / diag, 0.0)
        ew[e] = scale
        scale = 0.5 * scale
        for i, side in enumerate(sides):
            coef[i, e] = jnp.where(inside[side], scale * (sig + others[i]), 0.0)
        coef[4, e] = scale * (sig + below)
        coef[5, e] = scale * (sig + above)
        return carry

    lax.fori_loop(0, depth + 4, coefficients, 0)

    def around(e, values, s, offset):
        v = e - offset
        center = values[s, v]
        total = coef[4, e] * values[s, v - 1] + coef[5, e] * values[s, v + 1]
        for i, side in enumerate(sides):
            total = total + coef[i, e] * shifted(center, side)
        return center, total

    faces = ((0, -1), (depth - 1, depth))

    def face_weights(own, other):
        return 0.5 * (sg[own + 3] + sg[other + 3]), 0.5 * (pe[own + 1] + pe[other + 1])

    for k in range(1, depth - 1):
        for s in range(sources):
            i1[s, k + 2] = KEEP * ie[s, k + 1] + ew[k + 2] * nb[s, k]
    for own, other in faces:
        sig_w, pert_w = face_weights(own, other)
        for s in range(sources):
            moved = pert_w * fe[s, own + 1]
            st[s, own + 1] = st[s, own + 1] - moved
            st[s, other + 1] = moved
            i1[s, own + 2] = KEEP * ie[s, own + 1] + ew[own + 2] * (nb[s, own] - moved)
            i1[s, other + 2] = ew[other + 2] * (sig_w * ie[s, own + 1] + moved)
    for s in range(sources):
        i1[s, 0] = empty
        i1[s, depth + 3] = empty

    def second(e, carry):
        for s in range(sources):
            center, total = around(e, i1, s, 0)
            i2[s, e] = KEEP * center + ew[e] * st[s, e - 1] + total
        return carry

    lax.fori_loop(1, depth + 3, second, 0)
    for s in range(sources):
        i2[s, 0] = coef[5, 0] * i1[s, 1]
        i2[s, depth + 3] = coef[4, depth + 3] * i1[s, depth + 2]

    def pick(s):
        rows, _ = electrodes(s)
        value = i2[s].reshape((depth + 4) * nx, ny)
        high = value.astype(jnp.bfloat16)
        rest = value - high.astype(jnp.float32)
        middle = rest.astype(jnp.bfloat16)
        low = (rest - middle.astype(jnp.float32)).astype(jnp.bfloat16)
        columns = jnp.dot(
            jnp.concatenate([high, middle, low], axis=1), spot[s], preferred_element_type=jnp.float32)
        index = lax.broadcasted_iota(jnp.int32, columns.shape, 0)
        picked = jnp.sum(jnp.where(jnp.broadcast_to(rows, columns.shape) == index, columns, 0.0), axis=0, keepdims=True)
        reading = picked[:, :dipoles] - picked[:, dipoles:]
        for i in range(dipoles // 128):
            read[pl.ds(s * (dipoles // 128) + i, 1)] = reading[:, i * 128:(i + 1) * 128]

    for s in range(sources):
        pick(s)

    def spread(devices, source, target, send, recv):
        copies = []
        for i, device in enumerate(devices):
            copies.append(pltpu.make_async_remote_copy(
                src_ref=source(i), dst_ref=target.at[i], send_sem=send.at[i], recv_sem=recv.at[i],
                device_id=device, device_id_type=MESH))
            copies[-1].start()
        return copies

    pair_copies = spread([at(1, 0)], lambda i: read, got_pair, p_send, p_recv)
    pair_copies[0].wait_recv()
    part[...] = read[...] + got_pair[0]
    read_copies = spread(ring, lambda i: part, got, r_send, r_recv)

    arrived(edge_adj)
    begin(edge_inc)

    def adjoint_first(e, carry):
        for s in range(sources):
            center, total = around(e, ae, s, -1)
            a1[s, e] = KEEP * center + total
        return carry

    lax.fori_loop(0, depth + 4, adjoint_first, 0)

    def adjoint_second(e, carry):
        for s in range(sources):
            center, total = around(e, a1, s, 0)
            a2[s, e - 1] = KEEP * center + total
        return carry

    lax.fori_loop(1, depth + 3, adjoint_second, 0)

    for own, other in faces:
        lap[:, own] = lap[:, own] + (pe[own + 1] - pe[other + 1]).reshape(n_src, nx // n_src, ny)
    for k in range(depth - 1):
        face = (pe[k + 1] - pe[k + 2]).reshape(n_src, nx // n_src, ny)
        lap[:, k] = lap[:, k] + face
        lap[:, k + 1] = lap[:, k + 1] - face

    total = part[...]
    for i, copy in enumerate(read_copies):
        copy.wait_recv()
        total = total + got[i]
    for copy in pair_copies + read_copies:
        copy.wait_send()
    read[...] = total

    def scatter(s):
        per = dipoles // 128
        value = jnp.concatenate([read[pl.ds(s * per + i, 1)] for i in range(per)], axis=1) * weight_ref[pl.ds(s, 1)]
        value = jnp.concatenate([value, -value], axis=1)
        high = value.astype(jnp.bfloat16)
        low = (value - high.astype(jnp.float32)).astype(jnp.bfloat16)
        pieces = jnp.concatenate([spot[s, pl.ds(0, ny)] * high, spot[s, pl.ds(0, ny)] * low], axis=0)
        placed = lax.dot_general(hot[s], pieces, (((1,), (1,)), ((), ())), preferred_element_type=jnp.float32)
        placed = (placed[:, :ny] + placed[:, ny:]).reshape(depth + 4, nx, ny)
        b1[s] = ew[...] * placed

    for s in range(sources):
        scatter(s)

    def adjoint_readings(e, carry):
        for s in range(sources):
            center, total = around(e, b1, s, 0)
            a2[s, e - 1] = a2[s, e - 1] + (1.0 + KEEP) * center + total
        return carry

    lax.fori_loop(1, depth + 3, adjoint_readings, 0)

    arrived(edge_field)

    def across(k, carry):
        for s in range(sources):
            ns[s, k] = ns[s, k] + (fe[s, k] + fe[s, k + 2])
        return carry

    lax.fori_loop(0, depth, across, 0)

    def correlate(k, carry):
        product = empty
        mixed = empty
        for s in range(sources):
            adj, field = a2[s, k + 1], fe[s, k + 1]
            near_adj = a2[s, k] + a2[s, k + 2]
            for side in sides:
                near_adj = near_adj + neighbour(adj, side)
            product = product + adj * field
            mixed = mixed + (adj * ns[s, k] + field * near_adj)
            mixed = mixed - (a2[s, k] * fe[s, k] + a2[s, k + 2] * fe[s, k + 2])
        around_product = empty
        for side in sides:
            around_product = around_product + neighbour(product, side)
        result = (LEAKAGE + 3.0) * product + 0.5 * (around_product - mixed)
        co[:, k] = result.reshape(n_src, nx // n_src, ny)
        return carry

    lax.fori_loop(0, depth, correlate, 0)

    mate_copies = spread(mates, lambda i: co.at[mates[i][0]], rb, s_send, s_recv)

    arrived(edge_inc)
    for s in range(sources):
        for k in range(depth):
            o2[s, k] = i2[s, k + 2] + (ih[0, s, k] if k < 2 else ih[1, s, k + 2 - depth])
    store = pltpu.make_async_copy(o2, inc_hbm, out_sem)
    store.start()

    total = co[src]
    for i, copy in enumerate(mate_copies):
        copy.wait_recv()
        total = total + rb[i]
    hess_ref[...] = REGULARIZE * lap[src] - total

    for pair in (edge_sigma, edge_pert, edge_adj, edge_field, edge_inc):
        sent(pair)
    for copy in mate_copies:
        copy.wait_send()
    store.wait()


def on_device(conductivity, perturbation, fields, increment_start, adjoint_start, receivers, dipole_weight):
    sources, depth, nx, ny = fields.shape
    dipoles = dipole_weight.shape[1]
    n_src, n_gz = lax.axis_size("src"), lax.axis_size("gz")
    share = nx // n_src
    rows = sources * dipoles // 128

    def planes(*lead):
        return pltpu.VMEM((*lead, nx, ny), jnp.float32)

    others, mates = n_gz // 2 - 1, n_src - 1
    scratch = [
        pltpu.VMEM((sources, 2, dipoles), jnp.int32), pltpu.VMEM((sources, dipoles), jnp.float32),
        planes(depth + 6), planes(depth + 2), planes(sources, depth + 2), planes(sources, depth + 2),
        planes(sources, depth + 4), planes(sources, depth + 4), planes(sources, depth),
        planes(sources, depth + 6), planes(sources, depth + 4), planes(sources, depth + 2), planes(sources, depth + 4),
        planes(6, depth + 4), planes(depth + 4), planes(sources, depth), planes(sources, depth + 2),
        planes(2, sources, 2), planes(sources, depth), pltpu.VMEM((n_src, depth, share, ny), jnp.float32),
        pltpu.VMEM((sources, (depth + 4) * nx, 2 * dipoles), jnp.bfloat16),
        pltpu.VMEM((sources, 3 * ny, 2 * dipoles), jnp.bfloat16),
        pltpu.VMEM((rows, 128), jnp.float32), pltpu.VMEM((1, rows, 128), jnp.float32),
        pltpu.VMEM((rows, 128), jnp.float32), pltpu.VMEM((others, rows, 128), jnp.float32),
        pltpu.VMEM((n_src, depth, share, ny), jnp.float32), pltpu.VMEM((mates, depth, share, ny), jnp.float32),
        DMA((7,)), DMA, pltpu.SemaphoreType.REGULAR((3,)), DMA((2, 5)), DMA((2, 5)), DMA((4,)), DMA((4,)), DMA((1,)), DMA((1,)), DMA((others,)), DMA((others,)),
        DMA((mates,)), DMA((mates,)),
    ]
    anywhere = pl.BlockSpec(memory_space=pltpu.HBM)
    vmem = pl.BlockSpec(memory_space=pltpu.VMEM)
    return pl.pallas_call(
        kernel,
        out_shape=(
            jax.ShapeDtypeStruct((depth, share, ny), jnp.float32),
            jax.ShapeDtypeStruct(increment_start.shape, jnp.float32),
        ),
        in_specs=[anywhere] * 7,
        out_specs=(vmem, anywhere),
        scratch_shapes=scratch,
        compiler_params=pltpu.CompilerParams(
            collective_id=0, has_side_effects=True, vmem_limit_bytes=63 * 2**20),
    )(conductivity, perturbation, fields, increment_start, adjoint_start, jnp.swapaxes(receivers, 1, 2), dipole_weight)


def solution(mesh):
    return jax.shard_map(
        on_device,
        mesh=mesh,
        in_specs=(
            P("gz", None, None),
            P("gz", None, None),
            P("src", "gz", None, None),
            P("src", "gz", None, None),
            P("src", "gz", None, None),
            P("src", None, None),
            P("src", None),
        ),
        out_specs=(P("gz", "src", None), P("src", "gz", None, None)),
        check_vma=False,
    )
```
